128 devices in a mesh: dp: 4 (over z), seq: 32 (over x, y, core).
Axes of the slice: x: 4, y: 4, z: 4, core: 2. Of those that a mesh axis runs over, the one named last changes fastest.
Arguments:
- tokens: bfloat16 [4, 32768, 768], P('dp', 'seq'), as said below
- cotangent: bfloat16 [4, 32768, 768], P('dp', 'seq'), may hold values from -0.015625 to 0.015625
- lengths: int32 [4], P('dp'), may hold values from 8192 to 32768, as said below
- w_qkv: bfloat16 [768, 2304], replicated, may hold values from -0.21875 to 0.21875
- w_out: bfloat16 [768, 768], replicated, may hold values from -0.21875 to 0.21875
Outputs:
- attended: bfloat16 [4, 32768, 768], P('dp', 'seq')
- grad_qkv: float32 [768, 2304], replicated
- grad_out: float32 [768, 768], replicated
The draws below stay inside these ranges and needn't reach their ends.
Inputs may be any that keep to these rules, and one draw needn't show every extreme that they name: `tokens`: tile embeddings. `lengths`: some slide of every draw fills all 32768 positions.
All inputs are finite; a program needn't handle non-finite values.
Results may differ from the reference program's by a relative error of at most 0.012.
The reference program's roundings to bfloat16 on the way (of `projected`, `prob_half`, `context`, `grad_ctx`, `dscore` and `grad_proj`) count: a program that leaves them out, or rounds other values in their place, can miss the bound.
Values may be sent and summed in bfloat16 or wider, within the bound.
A program may use at most 192 MiB of HBM per device.

```python
import jax
import jax.numpy as jnp
from jax import lax

D = 768
HEADS = 16
HEAD_DIM = 48
SEG = 1024
RATE = 16
SEQLEN = 32768
N_DP = 4


def draw_tokens(key, part):
    key = jax.random.fold_in(key, 11)
    first_key = jax.random.fold_in(key, 0)
    field_rows = jnp.clip(jax.random.normal(first_key, (N_DP, SEQLEN, D), jnp.float32), -6.0, 6.0)
    return field_rows.astype(jnp.bfloat16)


def draw_lengths(key, part):
    key = jax.random.fold_in(key, 5)
    first_key, second_key = jax.random.split(key)
    counts = jax.random.randint(first_key, (N_DP,), SEQLEN // 4, SEQLEN + 1)
    fullest = jax.random.randint(second_key, (), 0, N_DP)
    return jnp.where(jnp.arange(N_DP) == fullest, SEQLEN, counts).astype(jnp.int32)


def block_scale(own_key, dims, cuts, low, largest):
    def one(axis_at, shards_of):
        heights = jax.random.uniform(jax.random.fold_in(jax.random.fold_in(own_key, 6), axis_at), (shards_of,), jnp.float32, low / len(cuts), largest / len(cuts))
        return jnp.repeat(jnp.exp(heights), dims[axis_at] // shards_of).reshape((-1,) + (1,) * (len(dims) - axis_at - 1))

    loudness = one(*cuts[0])
    for cut in cuts[1:]:
        loudness = loudness * one(*cut)
    return loudness


def scatter_about(key, extent, scale, most, cuts=(), kind=jnp.bfloat16):
    drawn = scale * jax.random.normal(key, extent, jnp.float32)
    if cuts:
        drawn = drawn * block_scale(key, extent, cuts, -0.22, 0.18)
    return jnp.clip(drawn, -most, most).astype(kind)


def setup_inputs(seed: int = 0) -> dict:
    key_of = jax.random.split(jax.random.key(seed), 6)
    tokens = draw_tokens(jax.random.fold_in(key_of[5], 71), 0)
    cotangent = scatter_about(key_of[1], (N_DP, SEQLEN, D), ((N_DP * SEQLEN) ** -0.5), 0.015625, ((0, 4), (1, 32)))
    lengths = draw_lengths(jax.random.fold_in(key_of[5], 71), 0)
    w_qkv = scatter_about(key_of[3], (D, 3 * D), D ** -0.5, 0.21875)
    w_out = scatter_about(key_of[4], (D, D), D ** -0.5, 0.21875)
    return dict(tokens=tokens, cotangent=cotangent, lengths=lengths, w_qkv=w_qkv, w_out=w_out)


masked_score = -1e30


def batched(form, left, right):
    return jnp.einsum(form, left.astype(jnp.float32), right.astype(jnp.float32))


def pick_rows(field_rows, dilation):
    head_count = field_rows.shape[0]
    folded = field_rows.reshape((head_count, field_rows.shape[1] // dilation, dilation) + field_rows.shape[2:])
    return jnp.stack([folded[head_idx, :, head_idx % dilation] for head_idx in range(head_count)])


def place_rows(sparse, dilation, fill_value):
    head_count = sparse.shape[0]
    select = jnp.arange(dilation, dtype=jnp.int32)[None, :] == (jnp.arange(head_count, dtype=jnp.int32) % dilation)[:, None]
    extra_dims = sparse.ndim - 2
    select = select.reshape((head_count, 1, dilation) + (1,) * extra_dims)
    spread = jnp.where(select, jnp.expand_dims(sparse, 2), fill_value)
    return spread.reshape((head_count, sparse.shape[1] * dilation) + sparse.shape[2:])


def local_forward(query_head, key_head, value_head, key_valid, glob_max, glob_total, score_scale):
    scores = score_scale * batched("sqe,ske->sqk", query_head, key_head)
    scores = jnp.where(key_valid[:, None, :], scores, masked_score)
    row_max = jnp.max(scores, axis=-1)
    row_total = jnp.sum(jnp.exp(scores - row_max[..., None]), axis=-1)
    top_score = jnp.maximum(row_max, glob_max)
    combined = row_total * jnp.exp(row_max - top_score) + glob_total * jnp.exp(glob_max - top_score)
    log_total = top_score + jnp.log(combined)
    prob_half = jnp.exp(scores - log_total[..., None]).astype(jnp.bfloat16)
    return log_total, batched("sqk,ske->sqe", prob_half, value_head)


def local_backward(query_head, key_head, value_head, key_valid, log_total, grad_head, delta_rows, score_scale):
    scores = score_scale * batched("sqe,ske->sqk", query_head, key_head)
    scores = jnp.where(key_valid[:, None, :], scores, masked_score)
    probs = jnp.exp(scores - log_total[..., None])
    prob_half = probs.astype(jnp.bfloat16)
    dprob = batched("sqe,ske->sqk", grad_head, value_head)
    dscore = (probs * (dprob - delta_rows[..., None])).astype(jnp.bfloat16)
    grad_q = score_scale * batched("sqk,ske->sqe", dscore, key_head)
    grad_k = score_scale * batched("sqk,sqe->ske", dscore, query_head)
    grad_v = batched("sqk,sqe->ske", prob_half, grad_head)
    return grad_q, grad_k, grad_v


def reference(tokens, cotangent, lengths, w_qkv, w_out):
    score_scale = HEAD_DIM ** -0.5
    offsets = jnp.arange(HEADS, dtype=jnp.int32) % RATE
    attended_all = []
    grad_qkv = jnp.zeros((D, 3 * D), jnp.float32)
    grad_out = jnp.zeros((D, D), jnp.float32)
    for slide_idx in range(N_DP):
        token_rows = tokens[slide_idx]
        cot_rows = cotangent[slide_idx]
        length = lengths[slide_idx]
        seq_total = token_rows.shape[0]
        segments = seq_total // SEG
        row_valid = jnp.arange(seq_total, dtype=jnp.int32) < length
        projected = jnp.dot(token_rows, w_qkv, preferred_element_type=jnp.float32).astype(jnp.bfloat16)
        per_head = projected.reshape(seq_total, 3, HEADS, HEAD_DIM).transpose(1, 2, 0, 3)
        queries, key_rows, value_rows = per_head[0], per_head[1], per_head[2]
        sparse_q = pick_rows(queries, RATE)
        sparse_k = pick_rows(key_rows, RATE)
        sparse_v = pick_rows(value_rows, RATE)
        sparse_count = seq_total // RATE
        sparse_pos = jnp.arange(sparse_count, dtype=jnp.int32)[None, :] * RATE + offsets[:, None]
        sparse_valid = sparse_pos < length
        glob_scores = score_scale * batched("hqe,hke->hqk", sparse_q, sparse_k)
        glob_scores = jnp.where(sparse_valid[:, None, :], glob_scores, masked_score)
        glob_max = jnp.max(glob_scores, axis=-1)
        glob_total = jnp.sum(jnp.exp(glob_scores - glob_max[..., None]), axis=-1)

        def seg_view(array_in):
            return array_in.reshape((HEADS, segments, SEG) + array_in.shape[2:])

        key_valid = row_valid.reshape(segments, SEG)
        full_max = place_rows(glob_max, RATE, masked_score)
        full_total = place_rows(glob_total, RATE, 0.0)

        def forward_head(items):
            return local_forward(items[0], items[1], items[2], key_valid, items[3], items[4], score_scale)

        log_total, out_local = lax.map(forward_head, (seg_view(queries), seg_view(key_rows), seg_view(value_rows), seg_view(full_max), seg_view(full_total)))
        log_total = log_total.reshape(HEADS, seq_total)
        out_local = out_local.reshape(HEADS, seq_total, HEAD_DIM)
        sparse_lse = pick_rows(log_total, RATE)
        glob_probs = jnp.exp(glob_scores - sparse_lse[..., None])
        glob_half = glob_probs.astype(jnp.bfloat16)
        glob_out = batched("hqk,hke->hqe", glob_half, sparse_v)
        out_full = out_local + place_rows(glob_out, RATE, 0.0)
        context = (out_full * row_valid[None, :, None]).astype(jnp.bfloat16)
        ctx_rows = context.transpose(1, 0, 2).reshape(seq_total, D)
        attended_all.append(jnp.dot(ctx_rows, w_out, preferred_element_type=jnp.float32).astype(jnp.bfloat16))

        grad_ctx = (jnp.dot(cot_rows, w_out.T, preferred_element_type=jnp.float32) * row_valid[:, None]).astype(jnp.bfloat16)
        grad_out = grad_out + jnp.dot(ctx_rows.T, cot_rows, preferred_element_type=jnp.float32)
        grad_heads = grad_ctx.reshape(seq_total, HEADS, HEAD_DIM).transpose(1, 0, 2)
        delta_rows = jnp.sum(grad_heads.astype(jnp.float32) * out_full, axis=-1)

        def backward_head(items):
            return local_backward(items[0], items[1], items[2], key_valid, items[3], items[4], items[5], score_scale)

        local_dq, local_dk, local_dv = lax.map(backward_head, (seg_view(queries), seg_view(key_rows), seg_view(value_rows), seg_view(log_total), seg_view(grad_heads), seg_view(delta_rows)))
        sparse_grad = pick_rows(grad_heads, RATE)
        sparse_delta = pick_rows(delta_rows, RATE)
        glob_dprob = batched("hqe,hke->hqk", sparse_grad, sparse_v)
        glob_dscore = (glob_probs * (glob_dprob - sparse_delta[..., None])).astype(jnp.bfloat16)
        glob_dq = score_scale * batched("hqk,hke->hqe", glob_dscore, sparse_k)
        glob_dk = score_scale * batched("hqk,hqe->hke", glob_dscore, sparse_q)
        glob_dv = batched("hqk,hqe->hke", glob_half, sparse_grad)
        shape_full = (HEADS, seq_total, HEAD_DIM)
        grad_q = local_dq.reshape(shape_full) + place_rows(glob_dq, RATE, 0.0)
        grad_k = local_dk.reshape(shape_full) + place_rows(glob_dk, RATE, 0.0)
        grad_v = local_dv.reshape(shape_full) + place_rows(glob_dv, RATE, 0.0)
        grad_proj = jnp.concatenate([grad_part.transpose(1, 0, 2).reshape(seq_total, D) for grad_part in (grad_q, grad_k, grad_v)], axis=1).astype(jnp.bfloat16)
        grad_qkv = grad_qkv + jnp.dot(token_rows.T, grad_proj, preferred_element_type=jnp.float32)
    return jnp.stack(attended_all), grad_qkv, grad_out
```

```python
import functools
import math

import jax
import jax.numpy as jnp
from jax import lax
from jax.experimental import pallas as pl
from jax.experimental.pallas import tpu as pltpu
from jax.sharding import PartitionSpec as P

D = 768
HEADS = 16
HEAD_DIM = 48
SEG = 1024
RATE = 16
ROWS = SEG // RATE
CHUNK = 256
SCALE = HEAD_DIM ** -0.5
SCALE2 = SCALE * math.log2(math.e)
MASKED = -1e30
MESH_ID = pl.DeviceIdType.MESH
F32 = jnp.float32
BF16 = jnp.bfloat16
VMEM_LIMIT = 56 * 2**20


def dot(left, right, left_dim, right_dim):
    return lax.dot_general(
        left, right, (((left_dim,), (right_dim,)), ((), ())), preferred_element_type=F32
    )


def three_parts(x):
    hi = x.astype(BF16).astype(F32)
    rest = x - hi
    mid = rest.astype(BF16).astype(F32)
    return hi, mid, (rest - mid).astype(BF16).astype(F32)


def row_select(head):
    row = lax.broadcasted_iota(jnp.int32, (ROWS, SEG), 0)
    col = lax.broadcasted_iota(jnp.int32, (ROWS, SEG), 1)
    return jnp.where(col == row * RATE + head, 1.0, 0.0).astype(BF16)


def one_rows():
    row = lax.broadcasted_iota(jnp.int32, (16, SEG), 0)
    return jnp.where(row == 0, 1.0, 0.0).astype(BF16)


def sparse_body(q_ref, k_ref, v_ref, g_ref, bias_ref, kv_ref, qg_ref):
    head = pl.program_id(0)
    select = row_select(head)
    blank = jnp.zeros((16, SEG), BF16)
    key_side = jnp.concatenate([k_ref[...], v_ref[...], bias_ref[...], blank], axis=0)
    query_side = jnp.concatenate([q_ref[...], g_ref[...], one_rows(), blank], axis=0)
    kv_ref[0] = dot(select, key_side, 1, 1).astype(BF16)
    qg = dot(select, query_side, 1, 1)
    lane = lax.broadcasted_iota(jnp.int32, (ROWS, 128), 1)
    query = jnp.where((lane < 48) | (lane == 96), qg, 0.0).astype(BF16)
    grad = jnp.where((lane >= 48) & (lane < 96), qg, 0.0).astype(BF16)
    scores = dot(query, key_side, 1, 0)
    top = jnp.max(scores, axis=1, keepdims=True)
    weight = jnp.exp2(scores * SCALE2 - top * SCALE2)
    total = jnp.sum(weight, axis=1, keepdims=True)
    delta = jnp.sum(weight * dot(grad, key_side, 1, 0), axis=1, keepdims=True)
    at = 97
    for value in (top * SCALE, total, delta):
        for part in three_parts(value):
            qg = jnp.where(lane == at, part, qg)
            at += 1
    qg_ref[0] = qg.astype(BF16)


def dilated_body(kv_ref, qg_ref, back_ref, key_ref, acc):
    step = pl.program_id(0)
    kv = kv_ref[...]
    qg = qg_ref[...]
    lane = lax.broadcasted_iota(jnp.int32, (CHUNK, 128), 1)
    zero = jnp.zeros_like(qg)
    query = jnp.where((lane < 48) | (lane == 96), qg, zero)
    grad = jnp.where((lane >= 48) & (lane < 96), qg, zero)
    flipped = qg.astype(F32).T
    loc_max = flipped[97:98] + flipped[98:99] + flipped[99:100]
    loc_sum = flipped[100:101] + flipped[101:102] + flipped[102:103]
    loc_delta = flipped[103:104] + flipped[104:105] + flipped[105:106]
    scores = dot(kv, query, 1, 1)
    raw_max = jnp.max(scores, axis=0, keepdims=True)
    weight = jnp.exp2(scores * SCALE2 - raw_max * SCALE2)
    glob_sum = jnp.sum(weight, axis=0, keepdims=True)
    glob_max = raw_max * SCALE
    top = jnp.maximum(glob_max, loc_max)
    log_total = top + jnp.log(
        loc_sum * jnp.exp(loc_max - top) + glob_sum * jnp.exp(glob_max - top)
    )
    probs = weight * jnp.exp(glob_max - log_total)
    half = probs.astype(BF16)
    out = dot(kv, half, 0, 0)
    delta = jnp.sum(out[48:96] * flipped[48:96], axis=0, keepdims=True)
    delta = delta + loc_delta * jnp.exp(loc_max - log_total)
    dscore = (probs * (dot(kv, grad, 1, 1) - delta)).astype(BF16)
    grad_q = dot(kv, dscore, 0, 0)
    row = lax.broadcasted_iota(jnp.int32, (128, CHUNK), 0)
    hi, mid, low = three_parts(log_total)
    back = jnp.where(row < 48, grad_q, jnp.where(row < 96, out, 0.0))
    back = jnp.where(row == 96, hi, jnp.where(row == 97, mid, jnp.where(row == 98, low, back)))
    back_ref[...] = back.T.astype(BF16)
    key_lane = lax.broadcasted_iota(jnp.int32, (kv.shape[0], 128), 1)
    term = jnp.where(
        key_lane < 48, dot(dscore, qg, 1, 0), jnp.where(key_lane < 96, dot(half, qg, 1, 0), 0.0)
    )

    @pl.when(step == 0)
    def _():
        acc[...] = term

    @pl.when(step > 0)
    def _():
        acc[...] += term

    @pl.when(step == pl.num_programs(0) - 1)
    def _():
        key_ref[...] = acc[...].astype(BF16)


def local_body(
    q_ref, k_ref, v_ref, g_ref, bias_ref, valid_ref, back_ref, key_ref,
    ctx_ref, dq_ref, dk_ref, dv_ref,
):
    head = pl.program_id(0)
    queries, keys, values, grads = q_ref[...], k_ref[...], v_ref[...], g_ref[...]
    keys_more = jnp.concatenate([keys, bias_ref[...]], axis=0)
    queries_more = jnp.concatenate([queries, one_rows()], axis=0)
    select = row_select(head)
    placed = dot(back_ref[0], select, 0, 0)
    key_back = jnp.concatenate([key_ref[0], key_ref[1]], axis=0)
    key_placed = dot(key_back, jnp.concatenate([select, select], axis=0), 0, 0)
    grad_k = key_placed[0:48]
    grad_v = key_placed[48:96]
    known = placed[96:97] + placed[97:98] + placed[98:99]
    position = lax.broadcasted_iota(jnp.int32, (1, CHUNK), 1)
    for at in range(0, SEG, CHUNK):
        cut = slice(at, at + CHUNK)
        scores = dot(keys_more, queries_more[:, cut], 0, 0)
        top = jnp.max(scores, axis=0, keepdims=True)
        weight = jnp.exp2(scores * SCALE2 - top * SCALE2)
        total = jnp.sum(weight, axis=0, keepdims=True)
        factor = jnp.where(
            position % RATE == head, jnp.exp(top * SCALE - known[:, cut]), 1.0 / total
        )
        probs = weight * factor
        half = probs.astype(BF16)
        out = dot(values, half, 1, 0) + placed[48:96, cut]
        grad = grads[:, cut]
        delta = jnp.sum(grad.astype(F32) * out, axis=0, keepdims=True)
        ctx_ref[:, cut] = (out * valid_ref[:, cut]).astype(BF16)
        dscore = (probs * (dot(values, grad, 0, 0) - delta)).astype(BF16)
        grad_q = dot(keys, dscore, 1, 0) + placed[0:48, cut]
        dq_ref[:, cut] = (grad_q * SCALE).astype(BF16)
        grad_k = grad_k + dot(queries[:, cut], dscore, 1, 1)
        grad_v = grad_v + dot(grad, half, 1, 1)
    dk_ref[...] = (grad_k * SCALE).astype(BF16)
    dv_ref[...] = grad_v.astype(BF16)


def exchange_body(per_chip, wide_ref, narrow_ref, wide_out, narrow_out, sem, wide_send, wide_recv, narrow_send, narrow_recv):
    me = lax.axis_index("seq")
    dp = lax.axis_index("dp")
    count = lax.axis_size("seq")
    chips = count // 2
    chip = me // 2
    core = me % 2

    def wide_at(target):
        return wide_ref.at[target // 2 if per_chip else target]

    barrier = pltpu.get_barrier_semaphore()

    def greet(step, carry):
        pl.semaphore_signal(
            barrier, inc=1, device_id=(dp, (me + step) % count), device_id_type=MESH_ID
        )
        return carry

    lax.fori_loop(1, count, greet, 0)
    own_wide = pltpu.make_async_copy(wide_at(me), wide_out.at[me], sem.at[0])
    own_narrow = pltpu.make_async_copy(narrow_ref.at[chip], narrow_out.at[chip], sem.at[1])
    own_wide.start()
    own_narrow.start()
    pl.semaphore_wait(barrier, count - 1)

    def wide_copy(step):
        target = (me + step) % count
        return pltpu.make_async_remote_copy(
            src_ref=wide_at(target), dst_ref=wide_out.at[me],
            send_sem=wide_send.at[step], recv_sem=wide_recv.at[step],
            device_id=(dp, target), device_id_type=MESH_ID,
        )

    def narrow_copy(step):
        target = (chip + step) % chips
        return pltpu.make_async_remote_copy(
            src_ref=narrow_ref.at[target], dst_ref=narrow_out.at[chip],
            send_sem=narrow_send.at[step], recv_sem=narrow_recv.at[step],
            device_id=(dp, target * 2 + core), device_id_type=MESH_ID,
        )

    def start_narrow(step, carry):
        narrow_copy(step).start()
        return carry

    def start_wide(step, carry):
        wide_copy(step).start()
        return carry

    def end_narrow(step, carry):
        narrow_copy(step).wait()
        return carry

    def end_wide(step, carry):
        wide_copy(step).wait()
        return carry

    lax.fori_loop(1, chips, start_narrow, 0)
    lax.fori_loop(1, count, start_wide, 0)
    lax.fori_loop(1, chips, end_narrow, 0)
    lax.fori_loop(1, count, end_wide, 0)
    own_wide.wait()
    own_narrow.wait()


def exchange(wide, narrow, per_chip, collective_id):
    count = lax.axis_size("seq")
    chips = count // 2
    return pl.pallas_call(
        functools.partial(exchange_body, per_chip),
        out_shape=(
            jax.ShapeDtypeStruct((count, ROWS, 128), BF16),
            jax.ShapeDtypeStruct((chips, ROWS, 128), BF16),
        ),
        in_specs=[pl.BlockSpec(memory_space=pltpu.VMEM)] * 2,
        out_specs=[pl.BlockSpec(memory_space=pltpu.VMEM)] * 2,
        scratch_shapes=[
            pltpu.SemaphoreType.DMA((2,)),
            pltpu.SemaphoreType.DMA((count,)),
            pltpu.SemaphoreType.DMA((count,)),
            pltpu.SemaphoreType.DMA((chips,)),
            pltpu.SemaphoreType.DMA((chips,)),
        ],
        compiler_params=pltpu.CompilerParams(
            collective_id=collective_id, has_side_effects=True, vmem_limit_bytes=16 * 2**20
        ),
    )(wide, narrow)


HALF = D // 2
PART = HALF // 3


def reduce_body(
    a_ref, b_ref, c_ref, d_ref, y_ref, x, pair, got1, sum1, got2, sum2, got3,
    load_sem, pair_send, pair_recv, send, recv,
):
    me = lax.axis_index("seq")
    z = lax.axis_index("dp")
    core = me % 2
    y = (me // 2) % 4
    xx = me // 8
    where = (xx, y, z)

    def peer(axis, coordinate):
        px, py, pz = [coordinate if axis == i else where[i] for i in range(3)]
        return (pz, (px * 4 + py) * 2 + core)

    partner = (z, me + 1 - 2 * core)
    barrier = pltpu.get_barrier_semaphore()
    pl.semaphore_signal(barrier, inc=1, device_id=partner, device_id_type=MESH_ID)
    for axis in range(3):
        for step in range(1, 4):
            pl.semaphore_signal(
                barrier, inc=1, device_id=peer(axis, (where[axis] + step) % 4), device_id_type=MESH_ID
            )
    loads = [
        pltpu.make_async_copy(ref, x.at[i], load_sem.at[i])
        for i, ref in enumerate((a_ref, b_ref, c_ref, d_ref))
    ]
    for load in loads:
        load.start()
    for load in loads:
        load.wait()
    pl.semaphore_wait(barrier, 10)

    mine = [core * HALF + part * PART for part in range(3)]
    other = [(1 - core) * HALF + part * PART for part in range(3)]

    def pair_copy(part):
        return pltpu.make_async_remote_copy(
            src_ref=x.at[:, pl.ds(pl.multiple_of(other[part], 128), PART)],
            dst_ref=pair.at[:, pl.ds(part * PART, PART)],
            send_sem=pair_send.at[part], recv_sem=pair_recv.at[part],
            device_id=partner, device_id_type=MESH_ID,
        )

    for part in range(3):
        pair_copy(part).start()

    axes = [(0, 1, 2), (1, 2, 0), (2, 0, 1)]
    first = [where[axes[p][0]] for p in range(3)]
    second = [where[axes[p][1]] for p in range(3)]
    third = [where[axes[p][2]] for p in range(3)]

    def remote(part, phase, step, src, dst, axis):
        target = (where[axis] + step) % 4
        return pltpu.make_async_remote_copy(
            src_ref=src, dst_ref=dst,
            send_sem=send.at[part, phase, step - 1], recv_sem=recv.at[part, phase, step - 1],
            device_id=peer(axis, target), device_id_type=MESH_ID,
        )

    def rows(start, size, unit):
        return pl.ds(pl.multiple_of(start, unit), size)

    def phase1(part, step):
        target = (first[part] + step) % 4
        return remote(part, 0, step, x.at[target, rows(mine[part], PART, 128)], got1.at[part, step - 1], axes[part][0])

    def phase2(part, step):
        target = (second[part] + step) % 4
        return remote(part, 1, step, sum1.at[part, rows(target * 32, 32, 32)], got2.at[part, step - 1], axes[part][1])

    def phase3(part, step):
        target = (third[part] + step) % 4
        return remote(
            part, 2, step,
            sum2.at[part, rows((target // 2) * 16, 16, 16), rows((target % 2) * 384, 384, 128)],
            got3.at[part, step - 1], axes[part][2],
        )

    for part in range(3):
        pair_copy(part).wait_recv()
        span = rows(mine[part], PART, 128)
        for i in range(4):
            x[i, span] = x[i, span] + pair[i, part * PART:(part + 1) * PART]
        for step in (2, 1, 3):
            phase1(part, step).start()
    for part in range(3):
        for step in (1, 2, 3):
            phase1(part, step).wait_recv()
        sum1[part] = (
            x[first[part], rows(mine[part], PART, 128)] + got1[part, 0] + got1[part, 1] + got1[part, 2]
        )
        for step in (2, 1, 3):
            phase2(part, step).start()
    for part in range(3):
        for step in (1, 2, 3):
            phase2(part, step).wait_recv()
        sum2[part] = (
            sum1[part, rows(second[part] * 32, 32, 32)] + got2[part, 0] + got2[part, 1] + got2[part, 2]
        )
        for step in (2, 1, 3):
            phase3(part, step).start()

    def shard3(part, owner):
        return y_ref.at[
            first[part],
            rows(mine[part] + second[part] * 32 + (owner // 2) * 16, 16, 16),
            rows((owner % 2) * 384, 384, 128),
        ]

    def shard2(part, owner):
        return y_ref.at[first[part], rows(mine[part] + owner * 32, 32, 32)]

    def shard1(part, owner):
        return y_ref.at[owner, rows(mine[part], PART, 128)]

    def gather(part, phase, step, shard, axis, arriving):
        owner = (where[axis] + (4 - step if arriving else 0)) % 4
        return remote(part, phase, step, shard(part, owner), shard(part, owner), axis)

    for part in range(3):
        for step in (1, 2, 3):
            phase3(part, step).wait_recv()
        own = third[part]
        total = (
            sum2[part, rows((own // 2) * 16, 16, 16), rows((own % 2) * 384, 384, 128)]
            + got3[part, 0] + got3[part, 1] + got3[part, 2]
        )
        y_ref[
            first[part],
            rows(mine[part] + second[part] * 32 + (own // 2) * 16, 16, 16),
            rows((own % 2) * 384, 384, 128),
        ] = total.astype(BF16)
        for step in (2, 1, 3):
            gather(part, 3, step, shard3, axes[part][2], False).start()
    for phase, shard, shard_next, at in ((3, shard3, shard2, 2), (4, shard2, shard1, 1)):
        for part in range(3):
            for step in (1, 2, 3):
                gather(part, phase, step, shard, axes[part][at], True).wait_recv()
            for step in (2, 1, 3):
                gather(part, phase + 1, step, shard_next, axes[part][at - 1], False).start()

    def pair_back(part, arriving):
        base = other[part] if arriving else mine[part]
        block = y_ref.at[:, rows(base, PART, 128)]
        return pltpu.make_async_remote_copy(
            src_ref=block, dst_ref=block,
            send_sem=pair_send.at[3 + part], recv_sem=pair_recv.at[3 + part],
            device_id=partner, device_id_type=MESH_ID,
        )

    for part in range(3):
        for step in (1, 2, 3):
            gather(part, 5, step, shard1, axes[part][0], True).wait_recv()
        pair_back(part, False).start()
    for part in range(3):
        pair_back(part, True).wait_recv()
    for part in range(3):
        pair_copy(part).wait_send()
        pair_back(part, False).wait_send()
        for step in (1, 2, 3):
            phase1(part, step).wait_send()
            phase2(part, step).wait_send()
            phase3(part, step).wait_send()
            gather(part, 3, step, shard3, axes[part][2], False).wait_send()
            gather(part, 4, step, shard2, axes[part][1], False).wait_send()
            gather(part, 5, step, shard1, axes[part][0], False).wait_send()


def reduce_all(arrays):
    return pl.pallas_call(
        reduce_body,
        out_shape=jax.ShapeDtypeStruct((4, D, D), BF16),
        in_specs=[pl.BlockSpec(memory_space=pl.ANY)] * 4,
        out_specs=pl.BlockSpec(memory_space=pltpu.VMEM),
        scratch_shapes=[
            pltpu.VMEM((4, D, D), F32),
            pltpu.VMEM((4, HALF, D), F32),
            pltpu.VMEM((3, 3, PART, D), F32),
            pltpu.VMEM((3, PART, D), F32),
            pltpu.VMEM((3, 3, 32, D), F32),
            pltpu.VMEM((3, 32, D), F32),
            pltpu.VMEM((3, 3, 16, 384), F32),
            pltpu.SemaphoreType.DMA((4,)),
            pltpu.SemaphoreType.DMA((6,)),
            pltpu.SemaphoreType.DMA((6,)),
            pltpu.SemaphoreType.DMA((3, 6, 3)),
            pltpu.SemaphoreType.DMA((3, 6, 3)),
        ],
        compiler_params=pltpu.CompilerParams(
            collective_id=2, has_side_effects=True, vmem_limit_bytes=VMEM_LIMIT
        ),
    )(*arrays)


def shards(tokens, cotangent, lengths, w_qkv, w_out):
    token_rows = tokens[0]
    cot_rows = cotangent[0]
    shard_count = lax.axis_size("seq")
    first_pos = lax.axis_index("seq") * SEG
    row_valid = first_pos + jnp.arange(SEG, dtype=jnp.int32) < lengths[0]
    valid = row_valid.astype(F32)[None, :]
    bias = jnp.where(
        (jnp.arange(16) == 0)[:, None] & ~row_valid[None, :], MASKED, 0.0
    ).astype(BF16)

    projected = dot(w_qkv, token_rows, 0, 1).astype(BF16)
    grad_ctx = (dot(w_out, cot_rows, 1, 1) * valid).astype(BF16)

    def head_block(offset):
        return pl.BlockSpec((HEAD_DIM, SEG), lambda h: (h + offset, 0))

    head_specs = [head_block(0), head_block(HEADS), head_block(2 * HEADS), head_block(0)]
    heads = (projected, projected, projected, grad_ctx)
    fixed_bias = pl.BlockSpec((16, SEG), lambda h: (0, 0))
    packed = pl.BlockSpec((1, ROWS, 128), lambda h: (h, 0, 0))
    packed_shape = jax.ShapeDtypeStruct((HEADS, ROWS, 128), BF16)
    kv, qg = pl.pallas_call(
        sparse_body,
        grid=(HEADS,),
        in_specs=head_specs + [fixed_bias],
        out_specs=[packed, packed],
        out_shape=[packed_shape, packed_shape],
        compiler_params=pltpu.CompilerParams(vmem_limit_bytes=VMEM_LIMIT),
    )(*heads, bias)

    kv_all, qg_all = exchange(kv, qg, True, 0)
    keys_total = shard_count * ROWS
    query_total = keys_total // 2
    chunk_spec = pl.BlockSpec((CHUNK, 128), lambda i: (i, 0))
    key_spec = pl.BlockSpec((keys_total, 128), lambda i: (0, 0))
    back, key_back = pl.pallas_call(
        dilated_body,
        grid=(query_total // CHUNK,),
        in_specs=[key_spec, chunk_spec],
        out_specs=[chunk_spec, key_spec],
        out_shape=[
            jax.ShapeDtypeStruct((query_total, 128), BF16),
            jax.ShapeDtypeStruct((keys_total, 128), BF16),
        ],
        scratch_shapes=[pltpu.VMEM((keys_total, 128), F32)],
        compiler_params=pltpu.CompilerParams(vmem_limit_bytes=VMEM_LIMIT),
    )(kv_all.reshape(keys_total, 128), qg_all.reshape(query_total, 128))
    key_own, back_own = exchange(
        key_back.reshape(shard_count, ROWS, 128), back.reshape(shard_count // 2, ROWS, 128), False, 1
    )

    out_block = pl.BlockSpec((HEAD_DIM, SEG), lambda h: (h, 0))
    out_shape = jax.ShapeDtypeStruct((D, SEG), BF16)
    context, grad_q, grad_k, grad_v = pl.pallas_call(
        local_body,
        grid=(HEADS,),
        in_specs=head_specs + [
            fixed_bias,
            pl.BlockSpec((1, SEG), lambda h: (0, 0)),
            packed,
            pl.BlockSpec((2, ROWS, 128), lambda h: (h, 0, 0)),
        ],
        out_specs=[out_block] * 4,
        out_shape=[out_shape] * 4,
        compiler_params=pltpu.CompilerParams(vmem_limit_bytes=VMEM_LIMIT),
    )(*heads, bias, valid, back_own, key_own)

    attended = dot(context, w_out, 0, 0).astype(BF16)
    terms = [dot(token_rows, part, 0, 1) for part in (grad_q, grad_k, grad_v)]
    terms.append(dot(context, cot_rows, 1, 0))
    total = reduce_all(terms)
    grad_qkv = jnp.concatenate([total[0], total[1], total[2]], axis=1).astype(F32)
    grad_out = total[3].astype(F32)
    return attended[None], grad_qkv, grad_out


def solution(mesh):
    return jax.shard_map(
        shards,
        mesh=mesh,
        in_specs=(P("dp", "seq", None), P("dp", "seq", None), P("dp"), P(), P()),
        out_specs=(P("dp", "seq", None), P(), P()),
        check_vma=False,
    )
```

```python
import functools
import math

import jax
import jax.numpy as jnp
from jax import lax
from jax.experimental import pallas as pl
from jax.experimental.pallas import tpu as pltpu
from jax.sharding import PartitionSpec as P

D = 768
HEADS = 16
HEAD_DIM = 48
SEG = 1024
RATE = 16
ROWS = SEG // RATE
CHUNK = 256
SCALE = HEAD_DIM ** -0.5
SCALE2 = SCALE * math.log2(math.e)
MASKED = -1e30
MESH_ID = pl.DeviceIdType.MESH
F32 = jnp.float32
BF16 = jnp.bfloat16
VMEM_LIMIT = 56 * 2**20


def dot(left, right, left_dim, right_dim):
    return lax.dot_general(
        left, right, (((left_dim,), (right_dim,)), ((), ())), preferred_element_type=F32
    )


def three_parts(x):
    hi = x.astype(BF16).astype(F32)
    rest = x - hi
    mid = rest.astype(BF16).astype(F32)
    return hi, mid, (rest - mid).astype(BF16).astype(F32)


def row_select(head):
    row = lax.broadcasted_iota(jnp.int32, (ROWS, SEG), 0)
    col = lax.broadcasted_iota(jnp.int32, (ROWS, SEG), 1)
    return jnp.where(col == row * RATE + head, 1.0, 0.0).astype(BF16)


def one_rows():
    row = lax.broadcasted_iota(jnp.int32, (16, SEG), 0)
    return jnp.where(row == 0, 1.0, 0.0).astype(BF16)


def sparse_body(q_ref, k_ref, v_ref, g_ref, bias_ref, kv_ref, qg_ref):
    head = pl.program_id(0)
    select = row_select(head)
    blank = jnp.zeros((16, SEG), BF16)
    key_side = jnp.concatenate([k_ref[...], v_ref[...], bias_ref[...], blank], axis=0)
    query_side = jnp.concatenate([q_ref[...], g_ref[...], one_rows(), blank], axis=0)
    kv_ref[0] = dot(select, key_side, 1, 1).astype(BF16)
    qg = dot(select, query_side, 1, 1)
    lane = lax.broadcasted_iota(jnp.int32, (ROWS, 128), 1)
    query = jnp.where((lane < 48) | (lane == 96), qg, 0.0).astype(BF16)
    grad = jnp.where((lane >= 48) & (lane < 96), qg, 0.0).astype(BF16)
    scores = dot(query, key_side, 1, 0)
    top = jnp.max(scores, axis=1, keepdims=True)
    weight = jnp.exp2(scores * SCALE2 - top * SCALE2)
    total = jnp.sum(weight, axis=1, keepdims=True)
    delta = jnp.sum(weight * dot(grad, key_side, 1, 0), axis=1, keepdims=True)
    at = 97
    for value in (top * SCALE, total, delta):
        for part in three_parts(value):
            qg = jnp.where(lane == at, part, qg)
            at += 1
    qg_ref[0] = qg.astype(BF16)


def dilated_body(kv_ref, qg_ref, back_ref, key_ref, acc):
    step = pl.program_id(0)
    kv = kv_ref[...]
    qg = qg_ref[...]
    lane = lax.broadcasted_iota(jnp.int32, (CHUNK, 128), 1)
    zero = jnp.zeros_like(qg)
    query = jnp.where((lane < 48) | (lane == 96), qg, zero)
    grad = jnp.where((lane >= 48) & (lane < 96), qg, zero)
    flipped = qg.astype(F32).T
    loc_max = flipped[97:98] + flipped[98:99] + flipped[99:100]
    loc_sum = flipped[100:101] + flipped[101:102] + flipped[102:103]
    loc_delta = flipped[103:104] + flipped[104:105] + flipped[105:106]
    scores = dot(kv, query, 1, 1)
    raw_max = jnp.max(scores, axis=0, keepdims=True)
    weight = jnp.exp2(scores * SCALE2 - raw_max * SCALE2)
    glob_sum = jnp.sum(weight, axis=0, keepdims=True)
    glob_max = raw_max * SCALE
    top = jnp.maximum(glob_max, loc_max)
    log_total = top + jnp.log(
        loc_sum * jnp.exp(loc_max - top) + glob_sum * jnp.exp(glob_max - top)
    )
    probs = weight * jnp.exp(glob_max - log_total)
    half = probs.astype(BF16)
    out = dot(kv, half, 0, 0)
    delta = jnp.sum(out[48:96] * flipped[48:96], axis=0, keepdims=True)
    delta = delta + loc_delta * jnp.exp(loc_max - log_total)
    dscore = (probs * (dot(kv, grad, 1, 1) - delta)).astype(BF16)
    grad_q = dot(kv, dscore, 0, 0)
    row = lax.broadcasted_iota(jnp.int32, (128, CHUNK), 0)
    hi, mid, low = three_parts(log_total)
    back = jnp.where(row < 48, grad_q, jnp.where(row < 96, out, 0.0))
    back = jnp.where(row == 96, hi, jnp.where(row == 97, mid, jnp.where(row == 98, low, back)))
    back_ref[...] = back.T.astype(BF16)
    key_lane = lax.broadcasted_iota(jnp.int32, (kv.shape[0], 128), 1)
    term = jnp.where(
        key_lane < 48, dot(dscore, qg, 1, 0), jnp.where(key_lane < 96, dot(half, qg, 1, 0), 0.0)
    )

    @pl.when(step == 0)
    def _():
        acc[...] = term

    @pl.when(step > 0)
    def _():
        acc[...] += term

    @pl.when(step == pl.num_programs(0) - 1)
    def _():
        key_ref[...] = acc[...].astype(BF16)


GROUPS = 4
GROUP_HEADS = HEADS // GROUPS
GROUP_ROWS = GROUP_HEADS * HEAD_DIM
PART = GROUP_ROWS // 3
LOCAL_CHUNK = 512


def local_head(head, q_ref, k_ref, v_ref, g_ref, bias_ref, valid_ref, back_ref, key_ref):
    queries, keys, values, grads = q_ref[...], k_ref[...], v_ref[...], g_ref[...]
    keys_more = jnp.concatenate([keys, bias_ref[...]], axis=0)
    queries_more = jnp.concatenate([queries, one_rows()], axis=0)
    select = row_select(head)
    placed = dot(back_ref[0], select, 0, 0)
    key_back = jnp.concatenate([key_ref[0], key_ref[1]], axis=0)
    key_placed = dot(key_back, jnp.concatenate([select, select], axis=0), 0, 0)
    known = placed[96:97] + placed[97:98] + placed[98:99]
    sparse = lax.broadcasted_iota(jnp.int32, (1, LOCAL_CHUNK), 1) % RATE == head

    def front(at):
        cut = slice(at, at + LOCAL_CHUNK)
        scores = dot(keys_more, queries_more[:, cut], 0, 0)
        top = jnp.max(scores, axis=0, keepdims=True)
        weight = jnp.exp2(scores * SCALE2 - top * SCALE2)
        total = jnp.sum(weight, axis=0, keepdims=True)
        return top, weight, total, dot(values, grads[:, cut], 0, 0)

    cuts = list(range(0, SEG, LOCAL_CHUNK))
    context, grad_q = [], []
    grad_k = grad_v = 0.0
    ready = front(cuts[0])
    for n, at in enumerate(cuts):
        top, weight, total, dprob = ready
        if n + 1 < len(cuts):
            ready = front(cuts[n + 1])
        cut = slice(at, at + LOCAL_CHUNK)
        factor = jnp.where(sparse, jnp.exp(top * SCALE - known[:, cut]), 1.0 / total)
        probs = weight * factor
        half = probs.astype(BF16)
        out = dot(values, half, 1, 0) + placed[48:96, cut]
        grad = grads[:, cut]
        delta = jnp.sum(grad.astype(F32) * out, axis=0, keepdims=True)
        context.append((out * valid_ref[:, cut]).astype(BF16))
        dscore = (probs * (dprob - delta)).astype(BF16)
        grad_q.append(((dot(keys, dscore, 1, 0) + placed[0:48, cut]) * SCALE).astype(BF16))
        grad_k = grad_k + dot(dscore, queries[:, cut], 1, 1)
        grad_v = grad_v + dot(half, grad, 1, 1)
    grad_k = ((grad_k.T + key_placed[0:48]) * SCALE).astype(BF16)
    grad_v = (grad_v.T + key_placed[48:96]).astype(BF16)
    return (
        jnp.concatenate(context, axis=1), jnp.concatenate(grad_q, axis=1), grad_k, grad_v
    )


def local_body(
    q_ref, k_ref, v_ref, g_ref, bias_ref, valid_ref, back_ref, key_ref, tok_ref, cot_ref, w_ref,
    att_ref, total_ref,
    rows_in, ctx, x, pair, got1, sum1, got2, got3, total,
    out_sem, pair_send, pair_recv, send, recv,
):
    head = pl.program_id(0)
    me = lax.axis_index("seq")
    z = lax.axis_index("dp")
    core = me % 2
    where = (me // 8, (me // 2) % 4, z)
    partner = (z, me + 1 - 2 * core)
    axes = [(0, 1, 2), (1, 2, 0), (2, 0, 1)]
    first = [where[axes[p][0]] for p in range(3)]
    second = [where[axes[p][1]] for p in range(3)]
    third = [where[axes[p][2]] for p in range(3)]
    parts, steps = range(3), (2, 1, 3)

    def peer(axis, coordinate):
        px, py, pz = [coordinate if axis == i else where[i] for i in range(3)]
        return (pz, (px * 4 + py) * 2 + core)

    def span(start, size, unit):
        return pl.ds(pl.multiple_of(start, unit), size)

    @pl.when(head == 0)
    def _():
        barrier = pltpu.get_barrier_semaphore()
        pl.semaphore_signal(barrier, inc=1, device_id=partner, device_id_type=MESH_ID)
        for axis in range(3):
            for step in range(1, 4):
                pl.semaphore_signal(
                    barrier, inc=1, device_id=peer(axis, (where[axis] + step) % 4), device_id_type=MESH_ID
                )
        pl.semaphore_wait(barrier, 10)

    def remote(g, part, phase, step, src, dst):
        axis = axes[part][(0, 1, 2, 1, 0)[phase]]
        return pltpu.make_async_remote_copy(
            src_ref=src, dst_ref=dst,
            send_sem=send.at[g, part, phase, step - 1], recv_sem=recv.at[g, part, phase, step - 1],
            device_id=peer(axis, (where[axis] + step) % 4), device_id_type=MESH_ID,
        )

    def pair_out(g):
        return pltpu.make_async_remote_copy(
            src_ref=x.at[g, pl.ds(2 * (1 - core), 2)], dst_ref=pair.at[g],
            send_sem=pair_send.at[g, 0], recv_sem=pair_recv.at[g, 0],
            device_id=partner, device_id_type=MESH_ID,
        )

    def pair_back(g, arriving):
        block = total.at[g, pl.ds(2 * ((1 - core) if arriving else core), 2)]
        return pltpu.make_async_remote_copy(
            src_ref=block, dst_ref=block,
            send_sem=pair_send.at[g, 1], recv_sem=pair_recv.at[g, 1],
            device_id=partner, device_id_type=MESH_ID,
        )

    def quarter1(part, a):
        return 2 * core + a // 2, span(part * PART + (a % 2) * 32, 32, 32)

    def quarter2(b):
        return span((b // 2) * 16, 16, 16), span((b % 2) * 384, 384, 128)

    def shard(part, b):
        array, _ = quarter1(part, first[part])
        return (
            array,
            span(part * PART + (first[part] % 2) * 32 + (b // 2) * 16, 16, 16),
            span((b % 2) * 384, 384, 128),
        )

    def phase1(g, part, step):
        array, rows = quarter1(part, (first[part] + step) % 4)
        return remote(g, part, 0, step, x.at[g, array, rows], got1.at[g, part, step - 1])

    def phase2(g, part, step):
        rows, cols = quarter2((second[part] + step) % 4)
        return remote(g, part, 1, step, sum1.at[g, part, rows, cols], got2.at[g, part, step - 1])

    def phase3(g, part, step, arriving=False):
        slot = got3.at[g, part, (third[part] + (4 - step if arriving else 0)) % 4]
        return remote(g, part, 2, step, slot, slot)

    def phase4(g, part, step, arriving=False):
        array, rows, cols = shard(part, (second[part] + (4 - step if arriving else 0)) % 4)
        block = total.at[g, array, rows, cols]
        return remote(g, part, 3, step, block, block)

    def phase5(g, part, step, arriving=False):
        array, rows = quarter1(part, (first[part] + (4 - step if arriving else 0)) % 4)
        block = total.at[g, array, rows]
        return remote(g, part, 4, step, block, block)

    def write_back(g):
        return pltpu.make_async_copy(total.at[g], total_ref.at[g], out_sem.at[g])

    def stage1(g):
        pair_out(g).wait_recv()
        for i in range(2):
            x[g, 2 * core + i] = x[g, 2 * core + i] + pair[g, i]
        for part in parts:
            for step in steps:
                phase1(g, part, step).start()
        pair_out(g).wait_send()

    def stage2(g):
        for part in parts:
            for step in steps:
                phase1(g, part, step).wait_recv()
            array, rows = quarter1(part, first[part])
            sum1[g, part] = x[g, array, rows] + got1[g, part, 0] + got1[g, part, 1] + got1[g, part, 2]
            for step in steps:
                phase2(g, part, step).start()
        for part in parts:
            for step in steps:
                phase1(g, part, step).wait_send()

    def stage3(g):
        for part in parts:
            for step in steps:
                phase2(g, part, step).wait_recv()
            rows, cols = quarter2(second[part])
            got3[g, part, third[part]] = (
                sum1[g, part, rows, cols] + got2[g, part, 0] + got2[g, part, 1] + got2[g, part, 2]
            )
            for step in steps:
                phase3(g, part, step).start()
        for part in parts:
            for step in steps:
                phase2(g, part, step).wait_send()

    def stage4(g):
        for part in parts:
            for step in steps:
                phase3(g, part, step, True).wait_recv()
            array, rows, cols = shard(part, second[part])
            total[g, array, rows, cols] = (
                got3[g, part, 0] + got3[g, part, 1] + got3[g, part, 2] + got3[g, part, 3]
            ).astype(BF16)
            for step in steps:
                phase4(g, part, step).start()
        for part in parts:
            for step in steps:
                phase3(g, part, step).wait_send()

    def stage5(g):
        for part in parts:
            for step in steps:
                phase4(g, part, step, True).wait_recv()
            for step in steps:
                phase5(g, part, step).start()
        for part in parts:
            for step in steps:
                phase4(g, part, step).wait_send()

    def stage6(g):
        for part in parts:
            for step in steps:
                phase5(g, part, step, True).wait_recv()
        pair_back(g, False).start()
        for part in parts:
            for step in steps:
                phase5(g, part, step).wait_send()

    def stage7(g):
        pair_back(g, True).wait_recv()
        write_back(g).start()
        pair_back(g, False).wait_send()

    stages = (stage1, stage2, stage3, stage4, stage5, stage6, stage7)

    context, grad_q, grad_k, grad_v = local_head(
        head, q_ref, k_ref, v_ref, g_ref, bias_ref, valid_ref, back_ref, key_ref
    )
    here = span((head % GROUP_HEADS) * HEAD_DIM, HEAD_DIM, 16)
    rows_in[0, here] = grad_q
    rows_in[1, here] = grad_k
    rows_in[2, here] = grad_v
    rows_in[3, here] = context
    ctx[span(head * HEAD_DIM, HEAD_DIM, 16)] = context

    @pl.when(head % GROUP_HEADS == GROUP_HEADS - 1)
    def _():
        g = head // GROUP_HEADS
        for i in range(4):
            x[g, i] = dot(rows_in[i], (cot_ref if i == 3 else tok_ref)[...], 1, 0)
        pair_out(g).start()

    for k, stage in enumerate(stages, 1):
        since = head - (GROUP_HEADS - 1) - k

        @pl.when((since >= 0) & (since % GROUP_HEADS == 0))
        def _(stage=stage, since=since):
            stage(since // GROUP_HEADS)

    @pl.when(head == HEADS - 1)
    def _():
        stage1(3)
        stage5(2)
        att_ref[...] = dot(ctx[...], w_ref[...], 0, 0).astype(BF16)
        stage2(3)
        stage6(2)
        stage3(3)
        stage7(2)
        stage4(3)
        stage5(3)
        stage6(3)
        stage7(3)
        for g in range(GROUPS):
            write_back(g).wait()


def exchange_body(per_chip, wide_ref, narrow_ref, wide_out, narrow_out, sem, wide_send, wide_recv, narrow_send, narrow_recv):
    me = lax.axis_index("seq")
    dp = lax.axis_index("dp")
    count = lax.axis_size("seq")
    chips = count // 2
    chip = me // 2
    core = me % 2

    def wide_at(target):
        return wide_ref.at[target // 2 if per_chip else target]

    barrier = pltpu.get_barrier_semaphore()

    def greet(step, carry):
        pl.semaphore_signal(
            barrier, inc=1, device_id=(dp, (me + step) % count), device_id_type=MESH_ID
        )
        return carry

    lax.fori_loop(1, count, greet, 0)
    own_wide = pltpu.make_async_copy(wide_at(me), wide_out.at[me], sem.at[0])
    own_narrow = pltpu.make_async_copy(narrow_ref.at[chip], narrow_out.at[chip], sem.at[1])
    own_wide.start()
    own_narrow.start()
    pl.semaphore_wait(barrier, count - 1)

    def wide_copy(step):
        target = (me + step) % count
        return pltpu.make_async_remote_copy(
            src_ref=wide_at(target), dst_ref=wide_out.at[me],
            send_sem=wide_send.at[step], recv_sem=wide_recv.at[step],
            device_id=(dp, target), device_id_type=MESH_ID,
        )

    def narrow_copy(step):
        target = (chip + step) % chips
        return pltpu.make_async_remote_copy(
            src_ref=narrow_ref.at[target], dst_ref=narrow_out.at[chip],
            send_sem=narrow_send.at[step], recv_sem=narrow_recv.at[step],
            device_id=(dp, target * 2 + core), device_id_type=MESH_ID,
        )

    def start_narrow(step, carry):
        narrow_copy(step).start()
        return carry

    def start_wide(step, carry):
        wide_copy(step).start()
        return carry

    def end_narrow(step, carry):
        narrow_copy(step).wait()
        return carry

    def end_wide(step, carry):
        wide_copy(step).wait()
        return carry

    lax.fori_loop(1, chips, start_narrow, 0)
    lax.fori_loop(1, count, start_wide, 0)
    lax.fori_loop(1, chips, end_narrow, 0)
    lax.fori_loop(1, count, end_wide, 0)
    own_wide.wait()
    own_narrow.wait()


def exchange(wide, narrow, per_chip, collective_id):
    count = lax.axis_size("seq")
    chips = count // 2
    return pl.pallas_call(
        functools.partial(exchange_body, per_chip),
        out_shape=(
            jax.ShapeDtypeStruct((count, ROWS, 128), BF16),
            jax.ShapeDtypeStruct((chips, ROWS, 128), BF16),
        ),
        in_specs=[pl.BlockSpec(memory_space=pltpu.VMEM)] * 2,
        out_specs=[pl.BlockSpec(memory_space=pltpu.VMEM)] * 2,
        scratch_shapes=[
            pltpu.SemaphoreType.DMA((2,)),
            pltpu.SemaphoreType.DMA((count,)),
            pltpu.SemaphoreType.DMA((count,)),
            pltpu.SemaphoreType.DMA((chips,)),
            pltpu.SemaphoreType.DMA((chips,)),
        ],
        compiler_params=pltpu.CompilerParams(
            collective_id=collective_id, has_side_effects=True, vmem_limit_bytes=16 * 2**20
        ),
    )(wide, narrow)


def shards(tokens, cotangent, lengths, w_qkv, w_out):
    token_rows = tokens[0]
    cot_rows = cotangent[0]
    shard_count = lax.axis_size("seq")
    first_pos = lax.axis_index("seq") * SEG
    row_valid = first_pos + jnp.arange(SEG, dtype=jnp.int32) < lengths[0]
    valid = row_valid.astype(F32)[None, :]
    bias = jnp.where(
        (jnp.arange(16) == 0)[:, None] & ~row_valid[None, :], MASKED, 0.0
    ).astype(BF16)

    projected = dot(w_qkv, token_rows, 0, 1).astype(BF16)
    grad_ctx = (dot(w_out, cot_rows, 1, 1) * valid).astype(BF16)

    def head_block(offset):
        return pl.BlockSpec((HEAD_DIM, SEG), lambda h: (h + offset, 0))

    head_specs = [head_block(0), head_block(HEADS), head_block(2 * HEADS), head_block(0)]
    heads = (projected, projected, projected, grad_ctx)
    fixed_bias = pl.BlockSpec((16, SEG), lambda h: (0, 0))
    packed = pl.BlockSpec((1, ROWS, 128), lambda h: (h, 0, 0))
    packed_shape = jax.ShapeDtypeStruct((HEADS, ROWS, 128), BF16)
    kv, qg = pl.pallas_call(
        sparse_body,
        grid=(HEADS,),
        in_specs=head_specs + [fixed_bias],
        out_specs=[packed, packed],
        out_shape=[packed_shape, packed_shape],
        compiler_params=pltpu.CompilerParams(vmem_limit_bytes=VMEM_LIMIT),
    )(*heads, bias)

    kv_all, qg_all = exchange(kv, qg, True, 0)
    keys_total = shard_count * ROWS
    query_total = keys_total // 2
    chunk_spec = pl.BlockSpec((CHUNK, 128), lambda i: (i, 0))
    key_spec = pl.BlockSpec((keys_total, 128), lambda i: (0, 0))
    back, key_back = pl.pallas_call(
        dilated_body,
        grid=(query_total // CHUNK,),
        in_specs=[key_spec, chunk_spec],
        out_specs=[chunk_spec, key_spec],
        out_shape=[
            jax.ShapeDtypeStruct((query_total, 128), BF16),
            jax.ShapeDtypeStruct((keys_total, 128), BF16),
        ],
        scratch_shapes=[pltpu.VMEM((keys_total, 128), F32)],
        compiler_params=pltpu.CompilerParams(vmem_limit_bytes=VMEM_LIMIT),
    )(kv_all.reshape(keys_total, 128), qg_all.reshape(query_total, 128))
    key_own, back_own = exchange(
        key_back.reshape(shard_count, ROWS, 128), back.reshape(shard_count // 2, ROWS, 128), False, 1
    )

    def whole(*shape):
        return pl.BlockSpec(shape, lambda h: (0,) * len(shape), pipeline_mode=pl.Buffered(1))

    attended, total = pl.pallas_call(
        local_body,
        grid=(HEADS,),
        in_specs=head_specs + [
            whole(16, SEG),
            whole(1, SEG),
            packed,
            pl.BlockSpec((2, ROWS, 128), lambda h: (h, 0, 0)),
            whole(SEG, D),
            whole(SEG, D),
            whole(D, D),
        ],
        out_specs=[whole(SEG, D), pl.BlockSpec(memory_space=pl.ANY)],
        out_shape=[
            jax.ShapeDtypeStruct((SEG, D), BF16),
            jax.ShapeDtypeStruct((GROUPS, 4, GROUP_ROWS, D), BF16),
        ],
        scratch_shapes=[
            pltpu.VMEM((4, GROUP_ROWS, SEG), BF16),
            pltpu.VMEM((D, SEG), BF16),
            pltpu.VMEM((GROUPS, 4, GROUP_ROWS, D), F32),
            pltpu.VMEM((GROUPS, 2, GROUP_ROWS, D), F32),
            pltpu.VMEM((GROUPS, 3, 3, 32, D), F32),
            pltpu.VMEM((GROUPS, 3, 32, D), F32),
            pltpu.VMEM((GROUPS, 3, 3, 16, 384), F32),
            pltpu.VMEM((GROUPS, 3, 4, 16, 384), F32),
            pltpu.VMEM((GROUPS, 4, GROUP_ROWS, D), BF16),
            pltpu.SemaphoreType.DMA((GROUPS,)),
            pltpu.SemaphoreType.DMA((GROUPS, 2)),
            pltpu.SemaphoreType.DMA((GROUPS, 2)),
            pltpu.SemaphoreType.DMA((GROUPS, 3, 5, 3)),
            pltpu.SemaphoreType.DMA((GROUPS, 3, 5, 3)),
        ],
        compiler_params=pltpu.CompilerParams(
            collective_id=2, has_side_effects=True, vmem_limit_bytes=60 * 2**20
        ),
    )(*heads, bias, valid, back_own, key_own, token_rows, cot_rows, w_out)

    grad_qkv = total[:, :3].transpose(3, 1, 0, 2).reshape(D, 3 * D).astype(F32)
    grad_out = total[:, 3].reshape(D, D).astype(F32)
    return attended[None], grad_qkv, grad_out


def solution(mesh):
    return jax.shard_map(
        shards,
        mesh=mesh,
        in_specs=(P("dp", "seq", None), P("dp", "seq", None), P("dp"), P(), P()),
        out_specs=(P("dp", "seq", None), P(), P()),
        check_vma=False,
    )
```

```python
import math

import jax
import jax.numpy as jnp
from jax import lax
from jax.experimental import pallas as pl
from jax.experimental.pallas import tpu as pltpu
from jax.sharding import PartitionSpec as P

D = 768
HEADS = 16
HEAD_DIM = 48
SEG = 1024
RATE = 16
ROWS = SEG // RATE
SCALE = HEAD_DIM ** -0.5
SCALE2 = SCALE * math.log2(math.e)
MASKED = -1e30
MESH_ID = pl.DeviceIdType.MESH
F32 = jnp.float32
BF16 = jnp.bfloat16
VMEM_LIMIT = 56 * 2**20


def dot(left, right, left_dim, right_dim):
    return lax.dot_general(
        left, right, (((left_dim,), (right_dim,)), ((), ())), preferred_element_type=F32
    )


def three_parts(x):
    hi = x.astype(BF16).astype(F32)
    rest = x - hi
    mid = rest.astype(BF16).astype(F32)
    return hi, mid, (rest - mid).astype(BF16).astype(F32)


def row_select(head):
    row = lax.broadcasted_iota(jnp.int32, (ROWS, SEG), 0)
    col = lax.broadcasted_iota(jnp.int32, (ROWS, SEG), 1)
    return jnp.where(col == row * RATE + head, 1.0, 0.0).astype(BF16)


def one_rows():
    row = lax.broadcasted_iota(jnp.int32, (16, SEG), 0)
    return jnp.where(row == 0, 1.0, 0.0).astype(BF16)


def dilated_body(
    proj_ref, grad_ref, bias_ref, back_out, key_out,
    msg, inbox, forwarded, acc, partial, back, key_half,
    send1, recv1, send2, recv2, send3, recv3, pair_send, pair_recv,
):
    me = lax.axis_index("seq")
    dp = lax.axis_index("dp")
    chips = HEADS
    chip = me // 2
    core = me % 2
    partner = (dp, me + 1 - 2 * core)
    barrier = pltpu.get_barrier_semaphore()
    pl.semaphore_signal(barrier, inc=1, device_id=partner, device_id_type=MESH_ID)

    def greet(step, carry):
        target = (chip + step) % chips
        pl.semaphore_signal(
            barrier, inc=1, device_id=(dp, target * 2 + core), device_id_type=MESH_ID
        )
        return carry

    lax.fori_loop(1, chips, greet, 0)
    pl.semaphore_wait(barrier, chips)

    def chip_copy(step, src, dst, send, recv):
        target = (chip + step) % chips
        return pltpu.make_async_remote_copy(
            src_ref=src(target), dst_ref=dst,
            send_sem=send.at[step], recv_sem=recv.at[step],
            device_id=(dp, target * 2 + core), device_id_type=MESH_ID,
        )

    def send_rows(step):
        return chip_copy(step, lambda t: msg.at[:, t], inbox.at[:, chip], send1, recv1)

    def send_back(step):
        return chip_copy(step, lambda t: back.at[t], back_out.at[chip], send2, recv2)

    def send_keys(step):
        return chip_copy(step, lambda t: key_half.at[t], key_out.at[chip], send3, recv3)

    def pair_copy(at, src, dst):
        return pltpu.make_async_remote_copy(
            src_ref=src, dst_ref=dst, send_sem=pair_send.at[at], recv_sem=pair_recv.at[at],
            device_id=partner, device_id_type=MESH_ID,
        )

    lane = lax.broadcasted_iota(jnp.int32, (ROWS, 128), 1)
    blank = jnp.zeros((16, SEG), BF16)
    ones = one_rows()
    bias = bias_ref[...]
    batch = 4

    def select_batch(at, carry):
        steps = [at * batch + i for i in range(batch)]
        heads = [(chip + step) % chips for step in steps]

        def rows(ref, offset, head):
            return ref[pl.ds(pl.multiple_of((offset + head) * HEAD_DIM, 16), HEAD_DIM)]

        key_sides = [
            jnp.concatenate([rows(proj_ref, HEADS, h), rows(proj_ref, 2 * HEADS, h), bias, blank], axis=0)
            for h in heads
        ]
        packed = [
            dot(
                row_select(h),
                jnp.concatenate([side, rows(proj_ref, 0, h), rows(grad_ref, 0, h), ones, blank], axis=0),
                1, 1,
            )
            for h, side in zip(heads, key_sides)
        ]
        queries = [p[:, 128:] for p in packed]
        both = [
            jnp.concatenate(
                [
                    jnp.where((lane < 48) | (lane == 96), q, 0.0).astype(BF16),
                    jnp.where((lane >= 48) & (lane < 96), q, 0.0).astype(BF16),
                ],
                axis=0,
            )
            for q in queries
        ]
        scored = [dot(b, side, 1, 0) for b, side in zip(both, key_sides)]
        tops = [jnp.max(r[:ROWS], axis=1, keepdims=True) for r in scored]
        weights = [jnp.exp2(r[:ROWS] * SCALE2 - top * SCALE2) for r, top in zip(scored, tops)]
        totals = [jnp.sum(w, axis=1, keepdims=True) for w in weights]
        deltas = [jnp.sum(w * r[ROWS:], axis=1, keepdims=True) for w, r in zip(weights, scored)]
        for h, p, q, top, total, delta in zip(heads, packed, queries, tops, totals, deltas):
            place = 97
            for value in (top * SCALE, total, delta):
                for part in three_parts(value):
                    q = jnp.where(lane == place, part, q)
                    place += 1
            msg[0, h] = p[:, :128].astype(BF16)
            msg[1, h] = q.astype(BF16)
        for step in steps:

            @pl.when(step > 0)
            def _(step=step):
                send_rows(step).start()

        return carry

    lax.fori_loop(0, chips // batch, select_batch, 0)
    inbox[0, chip] = msg[0, chip]
    inbox[1, chip] = msg[1, chip]

    def end_rows(step, carry):
        send_rows(step).wait()
        return carry

    lax.fori_loop(1, chips, end_rows, 0)
    forward = pair_copy(0, inbox.at[0], forwarded)
    forward.start()
    half_keys = chips * ROWS
    queries_in = inbox[1].reshape(half_keys, 128)
    kv_own = inbox[0].reshape(half_keys, 128)
    forward.wait()
    kv = jnp.concatenate([kv_own, forwarded[...].reshape(half_keys, 128)], axis=0)
    chunk = 512
    q_lane = lax.broadcasted_iota(jnp.int32, (chunk, 128), 1)
    row = lax.broadcasted_iota(jnp.int32, (128, chunk), 0)
    key_lane = lax.broadcasted_iota(jnp.int32, (2 * half_keys, 128), 1)

    def front(at):
        qg = queries_in[at:at + chunk]
        zero = jnp.zeros_like(qg)
        query = jnp.where((q_lane < 48) | (q_lane == 96), qg, zero)
        grad = jnp.where((q_lane >= 48) & (q_lane < 96), qg, zero)
        scores = dot(kv, query, 1, 1)
        raw_max = jnp.max(scores, axis=0, keepdims=True)
        weight = jnp.exp2(scores * SCALE2 - raw_max * SCALE2)
        return raw_max, weight, jnp.sum(weight, axis=0, keepdims=True), dot(kv, grad, 1, 1)

    cuts = list(range(0, half_keys, chunk))
    ready = front(cuts[0])
    for n, at in enumerate(cuts):
        raw_max, weight, glob_sum, dprob = ready
        if n + 1 < len(cuts):
            ready = front(cuts[n + 1])
        qg = queries_in[at:at + chunk]
        flipped = qg.astype(F32).T
        loc_max = flipped[97:98] + flipped[98:99] + flipped[99:100]
        loc_sum = flipped[100:101] + flipped[101:102] + flipped[102:103]
        loc_delta = flipped[103:104] + flipped[104:105] + flipped[105:106]
        glob_max = raw_max * SCALE
        top = jnp.maximum(glob_max, loc_max)
        log_total = top + jnp.log(
            loc_sum * jnp.exp(loc_max - top) + glob_sum * jnp.exp(glob_max - top)
        )
        probs = weight * jnp.exp(glob_max - log_total)
        half = probs.astype(BF16)
        out = dot(kv, half, 0, 0)
        delta = jnp.sum(out[48:96] * flipped[48:96], axis=0, keepdims=True)
        delta = delta + loc_delta * jnp.exp(loc_max - log_total)
        dscore = (probs * (dprob - delta)).astype(BF16)
        grad_q = dot(kv, dscore, 0, 0)
        hi, mid, low = three_parts(log_total)
        answer = jnp.where(row < 48, grad_q, jnp.where(row < 96, out, 0.0))
        answer = jnp.where(
            row == 96, hi, jnp.where(row == 97, mid, jnp.where(row == 98, low, answer))
        )
        back[at // ROWS:(at + chunk) // ROWS] = (
            answer.T.astype(BF16).reshape(chunk // ROWS, ROWS, 128)
        )
        term = jnp.where(
            key_lane < 48, dot(dscore, qg, 1, 0),
            jnp.where(key_lane < 96, dot(half, qg, 1, 0), 0.0),
        ).reshape(2, half_keys, 128)
        if n == 0:
            acc[...] = term
        else:
            acc[...] += term

    share = pair_copy(1, acc.at[1], partial)
    share.start()

    def start_back(step, carry):
        send_back(step).start()
        return carry

    lax.fori_loop(1, chips, start_back, 0)
    back_out[chip] = back[chip]
    share.wait()
    key_half[...] = (acc[0] + partial[...]).astype(BF16).reshape(chips, ROWS, 128)

    def start_keys(step, carry):
        send_keys(step).start()
        return carry

    lax.fori_loop(1, chips, start_keys, 0)
    key_out[chip] = key_half[chip]

    def end_back(step, carry):
        send_back(step).wait()
        send_keys(step).wait()
        return carry

    lax.fori_loop(1, chips, end_back, 0)


def dilated_level(projected, grad_ctx, bias):
    packed = jax.ShapeDtypeStruct((HEADS, ROWS, 128), BF16)
    half_keys = HEADS * ROWS
    semaphores = pltpu.SemaphoreType.DMA((HEADS,))
    return pl.pallas_call(
        dilated_body,
        out_shape=(packed, packed),
        in_specs=[pl.BlockSpec(memory_space=pltpu.VMEM)] * 3,
        out_specs=[pl.BlockSpec(memory_space=pltpu.VMEM)] * 2,
        scratch_shapes=[
            pltpu.VMEM((2, HEADS, ROWS, 128), BF16),
            pltpu.VMEM((2, HEADS, ROWS, 128), BF16),
            pltpu.VMEM((HEADS, ROWS, 128), BF16),
            pltpu.VMEM((2, half_keys, 128), F32),
            pltpu.VMEM((half_keys, 128), F32),
            pltpu.VMEM((HEADS, ROWS, 128), BF16),
            pltpu.VMEM((HEADS, ROWS, 128), BF16),
        ] + [semaphores] * 6 + [pltpu.SemaphoreType.DMA((2,))] * 2,
        compiler_params=pltpu.CompilerParams(
            collective_id=0, has_side_effects=True, vmem_limit_bytes=VMEM_LIMIT
        ),
    )(projected, grad_ctx, bias)


def finish_body(total_ref, last_ref, qkv_ref, out_ref):
    qkv_ref[...] = total_ref[:, 0].reshape(D, D).astype(F32).T

    @pl.when(pl.program_id(0) == 0)
    def _():
        out_ref[...] = last_ref[:, 0].reshape(D, D).astype(F32)


def finish(total):
    return pl.pallas_call(
        finish_body,
        grid=(3,),
        in_specs=[
            pl.BlockSpec((GROUPS, 1, GROUP_ROWS, D), lambda i: (0, i, 0, 0)),
            pl.BlockSpec((GROUPS, 1, GROUP_ROWS, D), lambda i: (0, 3, 0, 0)),
        ],
        out_specs=[pl.BlockSpec((D, D), lambda i: (0, i)), pl.BlockSpec((D, D), lambda i: (0, 0))],
        out_shape=[jax.ShapeDtypeStruct((D, 3 * D), F32), jax.ShapeDtypeStruct((D, D), F32)],
        compiler_params=pltpu.CompilerParams(vmem_limit_bytes=VMEM_LIMIT),
    )(total, total)


GROUPS = 4
GROUP_HEADS = HEADS // GROUPS
GROUP_ROWS = GROUP_HEADS * HEAD_DIM
PART = GROUP_ROWS // 3
LOCAL_CHUNK = 512


def local_head(head, q_ref, k_ref, v_ref, g_ref, bias_ref, valid_ref, back_ref, key_ref):
    queries, keys, values, grads = q_ref[...], k_ref[...], v_ref[...], g_ref[...]
    keys_more = jnp.concatenate([keys, bias_ref[...]], axis=0)
    queries_more = jnp.concatenate([queries, one_rows()], axis=0)
    select = row_select(head)
    placed = dot(back_ref[0], select, 0, 0)
    key_placed = dot(key_ref[0], select, 0, 0)
    known = placed[96:97] + placed[97:98] + placed[98:99]
    sparse = lax.broadcasted_iota(jnp.int32, (1, LOCAL_CHUNK), 1) % RATE == head

    def front(at):
        cut = slice(at, at + LOCAL_CHUNK)
        scores = dot(keys_more, queries_more[:, cut], 0, 0)
        top = jnp.max(scores, axis=0, keepdims=True)
        weight = jnp.exp2(scores * SCALE2 - top * SCALE2)
        total = jnp.sum(weight, axis=0, keepdims=True)
        return top, weight, total, dot(values, grads[:, cut], 0, 0)

    cuts = list(range(0, SEG, LOCAL_CHUNK))
    context, grad_q = [], []
    grad_k = grad_v = 0.0
    ready = front(cuts[0])
    for n, at in enumerate(cuts):
        top, weight, total, dprob = ready
        if n + 1 < len(cuts):
            ready = front(cuts[n + 1])
        cut = slice(at, at + LOCAL_CHUNK)
        factor = jnp.where(sparse, jnp.exp(top * SCALE - known[:, cut]), 1.0 / total)
        probs = weight * factor
        half = probs.astype(BF16)
        out = dot(values, half, 1, 0) + placed[48:96, cut]
        grad = grads[:, cut]
        delta = jnp.sum(grad.astype(F32) * out, axis=0, keepdims=True)
        context.append((out * valid_ref[:, cut]).astype(BF16))
        dscore = (probs * (dprob - delta)).astype(BF16)
        grad_q.append(((dot(keys, dscore, 1, 0) + placed[0:48, cut]) * SCALE).astype(BF16))
        grad_k = grad_k + dot(dscore, queries[:, cut], 1, 1)
        grad_v = grad_v + dot(half, grad, 1, 1)
    grad_k = ((grad_k.T + key_placed[0:48]) * SCALE).astype(BF16)
    grad_v = (grad_v.T + key_placed[48:96]).astype(BF16)
    return (
        jnp.concatenate(context, axis=1), jnp.concatenate(grad_q, axis=1), grad_k, grad_v
    )


def local_body(
    q_ref, k_ref, v_ref, g_ref, bias_ref, valid_ref, back_ref, key_ref, tok_ref, cot_ref, w_ref,
    att_ref, total_ref,
    rows_in, ctx, x, pair, got1, sum1, got2, got3, total,
    out_sem, pair_send, pair_recv, send, recv,
):
    head = pl.program_id(0)
    me = lax.axis_index("seq")
    z = lax.axis_index("dp")
    core = me % 2
    where = (me // 8, (me // 2) % 4, z)
    partner = (z, me + 1 - 2 * core)
    axes = [(0, 1, 2), (1, 2, 0), (2, 0, 1)]
    first = [where[axes[p][0]] for p in range(3)]
    second = [where[axes[p][1]] for p in range(3)]
    third = [where[axes[p][2]] for p in range(3)]
    parts, steps = range(3), (2, 1, 3)

    def peer(axis, coordinate):
        px, py, pz = [coordinate if axis == i else where[i] for i in range(3)]
        return (pz, (px * 4 + py) * 2 + core)

    def span(start, size, unit):
        return pl.ds(pl.multiple_of(start, unit), size)

    @pl.when(head == 0)
    def _():
        barrier = pltpu.get_barrier_semaphore()
        pl.semaphore_signal(barrier, inc=1, device_id=partner, device_id_type=MESH_ID)
        for axis in range(3):
            for step in range(1, 4):
                pl.semaphore_signal(
                    barrier, inc=1, device_id=peer(axis, (where[axis] + step) % 4), device_id_type=MESH_ID
                )
        pl.semaphore_wait(barrier, 10)

    def remote(g, part, phase, step, src, dst):
        axis = axes[part][(0, 1, 2, 1, 0)[phase]]
        return pltpu.make_async_remote_copy(
            src_ref=src, dst_ref=dst,
            send_sem=send.at[g, part, phase, step - 1], recv_sem=recv.at[g, part, phase, step - 1],
            device_id=peer(axis, (where[axis] + step) % 4), device_id_type=MESH_ID,
        )

    def pair_out(g):
        return pltpu.make_async_remote_copy(
            src_ref=x.at[g, pl.ds(2 * (1 - core), 2)], dst_ref=pair.at[g],
            send_sem=pair_send.at[g, 0], recv_sem=pair_recv.at[g, 0],
            device_id=partner, device_id_type=MESH_ID,
        )

    def pair_back(g, arriving):
        block = total.at[g, pl.ds(2 * ((1 - core) if arriving else core), 2)]
        return pltpu.make_async_remote_copy(
            src_ref=block, dst_ref=block,
            send_sem=pair_send.at[g, 1], recv_sem=pair_recv.at[g, 1],
            device_id=partner, device_id_type=MESH_ID,
        )

    def quarter1(part, a):
        return 2 * core + a // 2, span(part * PART + (a % 2) * 32, 32, 32)

    def quarter2(b):
        return span((b // 2) * 16, 16, 16), span((b % 2) * 384, 384, 128)

    def shard(part, b):
        array, _ = quarter1(part, first[part])
        return (
            array,
            span(part * PART + (first[part] % 2) * 32 + (b // 2) * 16, 16, 16),
            span((b % 2) * 384, 384, 128),
        )

    def phase1(g, part, step):
        array, rows = quarter1(part, (first[part] + step) % 4)
        return remote(g, part, 0, step, x.at[g, array, rows], got1.at[g, part, step - 1])

    def phase2(g, part, step):
        rows, cols = quarter2((second[part] + step) % 4)
        return remote(g, part, 1, step, sum1.at[g, part, rows, cols], got2.at[g, part, step - 1])

    def phase3(g, part, step, arriving=False):
        slot = got3.at[g, part, (third[part] + (4 - step if arriving else 0)) % 4]
        return remote(g, part, 2, step, slot, slot)

    def phase4(g, part, step, arriving=False):
        array, rows, cols = shard(part, (second[part] + (4 - step if arriving else 0)) % 4)
        block = total.at[g, array, rows, cols]
        return remote(g, part, 3, step, block, block)

    def phase5(g, part, step, arriving=False):
        array, rows = quarter1(part, (first[part] + (4 - step if arriving else 0)) % 4)
        block = total.at[g, array, rows]
        return remote(g, part, 4, step, block, block)

    def write_back(g):
        return pltpu.make_async_copy(total.at[g], total_ref.at[g], out_sem.at[g])

    def stage1(g):
        pair_out(g).wait_recv()
        for i in range(2):
            x[g, 2 * core + i] = x[g, 2 * core + i] + pair[g, i]
        for part in parts:
            for step in steps:
                phase1(g, part, step).start()
        pair_out(g).wait_send()

    def stage2(g):
        for part in parts:
            for step in steps:
                phase1(g, part, step).wait_recv()
            array, rows = quarter1(part, first[part])
            sum1[g, part] = x[g, array, rows] + got1[g, part, 0] + got1[g, part, 1] + got1[g, part, 2]
            for step in steps:
                phase2(g, part, step).start()
        for part in parts:
            for step in steps:
                phase1(g, part, step).wait_send()

    def stage3(g):
        for part in parts:
            for step in steps:
                phase2(g, part, step).wait_recv()
            rows, cols = quarter2(second[part])
            got3[g, part, third[part]] = (
                sum1[g, part, rows, cols] + got2[g, part, 0] + got2[g, part, 1] + got2[g, part, 2]
            )
            for step in steps:
                phase3(g, part, step).start()
        for part in parts:
            for step in steps:
                phase2(g, part, step).wait_send()

    def stage4(g):
        for part in parts:
            for step in steps:
                phase3(g, part, step, True).wait_recv()
            array, rows, cols = shard(part, second[part])
            total[g, array, rows, cols] = (
                got3[g, part, 0] + got3[g, part, 1] + got3[g, part, 2] + got3[g, part, 3]
            ).astype(BF16)
            for step in steps:
                phase4(g, part, step).start()
        for part in parts:
            for step in steps:
                phase3(g, part, step).wait_send()

    def stage5(g):
        for part in parts:
            for step in steps:
                phase4(g, part, step, True).wait_recv()
            for step in steps:
                phase5(g, part, step).start()
        for part in parts:
            for step in steps:
                phase4(g, part, step).wait_send()

    def stage6(g):
        for part in parts:
            for step in steps:
                phase5(g, part, step, True).wait_recv()
        pair_back(g, False).start()
        for part in parts:
            for step in steps:
                phase5(g, part, step).wait_send()

    def stage7(g):
        pair_back(g, True).wait_recv()
        write_back(g).start()
        pair_back(g, False).wait_send()

    stages = (stage1, stage2, stage3, stage4, stage5, stage6, stage7)

    context, grad_q, grad_k, grad_v = local_head(
        head, q_ref, k_ref, v_ref, g_ref, bias_ref, valid_ref, back_ref, key_ref
    )
    here = span((head % GROUP_HEADS) * HEAD_DIM, HEAD_DIM, 16)
    rows_in[0, here] = grad_q
    rows_in[1, here] = grad_k
    rows_in[2, here] = grad_v
    rows_in[3, here] = context
    ctx[span(head * HEAD_DIM, HEAD_DIM, 16)] = context

    @pl.when(head % GROUP_HEADS == GROUP_HEADS - 1)
    def _():
        g = head // GROUP_HEADS
        for i in range(4):
            x[g, i] = dot(rows_in[i], (cot_ref if i == 3 else tok_ref)[...], 1, 0)
        pair_out(g).start()

    for k, stage in enumerate(stages, 1):
        since = head - (GROUP_HEADS - 1) - k

        @pl.when((since >= 0) & (since % GROUP_HEADS == 0))
        def _(stage=stage, since=since):
            stage(since // GROUP_HEADS)

    @pl.when(head == HEADS - 1)
    def _():
        stage1(3)
        stage5(2)
        att_ref[...] = dot(ctx[...], w_ref[...], 0, 0).astype(BF16)
        stage2(3)
        stage6(2)
        stage3(3)
        stage7(2)
        stage4(3)
        stage5(3)
        stage6(3)
        stage7(3)
        for g in range(GROUPS):
            write_back(g).wait()


def shards(tokens, cotangent, lengths, w_qkv, w_out):
    token_rows = tokens[0]
    cot_rows = cotangent[0]
    first_pos = lax.axis_index("seq") * SEG
    row_valid = first_pos + jnp.arange(SEG, dtype=jnp.int32) < lengths[0]
    valid = row_valid.astype(F32)[None, :]
    bias = jnp.where(
        (jnp.arange(16) == 0)[:, None] & ~row_valid[None, :], MASKED, 0.0
    ).astype(BF16)

    projected = dot(w_qkv, token_rows, 0, 1).astype(BF16)
    grad_ctx = (dot(w_out, cot_rows, 1, 1) * valid).astype(BF16)

    def head_block(offset):
        return pl.BlockSpec((HEAD_DIM, SEG), lambda h: (h + offset, 0))

    head_specs = [head_block(0), head_block(HEADS), head_block(2 * HEADS), head_block(0)]
    heads = (projected, projected, projected, grad_ctx)
    packed = pl.BlockSpec((1, ROWS, 128), lambda h: (h, 0, 0))
    back_own, key_own = dilated_level(projected, grad_ctx, bias)

    def whole(*shape):
        return pl.BlockSpec(shape, lambda h: (0,) * len(shape), pipeline_mode=pl.Buffered(1))

    attended, total = pl.pallas_call(
        local_body,
        grid=(HEADS,),
        in_specs=head_specs + [
            whole(16, SEG),
            whole(1, SEG),
            packed,
            packed,
            whole(SEG, D),
            whole(SEG, D),
            whole(D, D),
        ],
        out_specs=[whole(SEG, D), pl.BlockSpec(memory_space=pl.ANY)],
        out_shape=[
            jax.ShapeDtypeStruct((SEG, D), BF16),
            jax.ShapeDtypeStruct((GROUPS, 4, GROUP_ROWS, D), BF16),
        ],
        scratch_shapes=[
            pltpu.VMEM((4, GROUP_ROWS, SEG), BF16),
            pltpu.VMEM((D, SEG), BF16),
            pltpu.VMEM((GROUPS, 4, GROUP_ROWS, D), F32),
            pltpu.VMEM((GROUPS, 2, GROUP_ROWS, D), F32),
            pltpu.VMEM((GROUPS, 3, 3, 32, D), F32),
            pltpu.VMEM((GROUPS, 3, 32, D), F32),
            pltpu.VMEM((GROUPS, 3, 3, 16, 384), F32),
            pltpu.VMEM((GROUPS, 3, 4, 16, 384), F32),
            pltpu.VMEM((GROUPS, 4, GROUP_ROWS, D), BF16),
            pltpu.SemaphoreType.DMA((GROUPS,)),
            pltpu.SemaphoreType.DMA((GROUPS, 2)),
            pltpu.SemaphoreType.DMA((GROUPS, 2)),
            pltpu.SemaphoreType.DMA((GROUPS, 3, 5, 3)),
            pltpu.SemaphoreType.DMA((GROUPS, 3, 5, 3)),
        ],
        compiler_params=pltpu.CompilerParams(
            collective_id=2, has_side_effects=True, vmem_limit_bytes=60 * 2**20
        ),
    )(*heads, bias, valid, back_own, key_own, token_rows, cot_rows, w_out)

    grad_qkv, grad_out = finish(total)
    return attended[None], grad_qkv, grad_out


def solution(mesh):
    return jax.shard_map(
        shards,
        mesh=mesh,
        in_specs=(P("dp", "seq", None), P("dp", "seq", None), P("dp"), P(), P()),
        out_specs=(P("dp", "seq", None), P(), P()),
        check_vma=False,
    )
```

```python
import math

import jax
import jax.numpy as jnp
from jax import lax
from jax.experimental import pallas as pl
from jax.experimental.pallas import tpu as pltpu
from jax.sharding import PartitionSpec as P

D = 768
HEADS = 16
HEAD_DIM = 48
SEG = 1024
RATE = 16
ROWS = SEG // RATE
SCALE = HEAD_DIM ** -0.5
SCALE2 = SCALE * math.log2(math.e)
MASKED = -1e30
MESH_ID = pl.DeviceIdType.MESH
F32 = jnp.float32
BF16 = jnp.bfloat16
VMEM_LIMIT = 56 * 2**20


def dot(left, right, left_dim, right_dim):
    return lax.dot_general(
        left, right, (((left_dim,), (right_dim,)), ((), ())), preferred_element_type=F32
    )


def three_parts(x):
    hi = x.astype(BF16).astype(F32)
    rest = x - hi
    mid = rest.astype(BF16).astype(F32)
    return hi, mid, (rest - mid).astype(BF16).astype(F32)


def row_select(head):
    row = lax.broadcasted_iota(jnp.int32, (ROWS, SEG), 0)
    col = lax.broadcasted_iota(jnp.int32, (ROWS, SEG), 1)
    return jnp.where(col == row * RATE + head, 1.0, 0.0).astype(BF16)


def one_rows():
    row = lax.broadcasted_iota(jnp.int32, (16, SEG), 0)
    return jnp.where(row == 0, 1.0, 0.0).astype(BF16)


def bias_rows(valid):
    row = lax.broadcasted_iota(jnp.int32, (16, SEG), 0)
    return jnp.where(row == 0, (1.0 - valid) * MASKED, 0.0).astype(BF16)


def dilated_body(
    proj_ref, cot_ref, w_ref, valid_ref, back_out, key_out, grad_ref,
    cot, weight_out, load_sem, msg, inbox, forwarded, acc, partial, back, key_half,
    send0, recv0, send1, recv1, send2, recv2, send3, recv3, pair_send, pair_recv,
):
    me = lax.axis_index("seq")
    dp = lax.axis_index("dp")
    chips = HEADS
    chip = me // 2
    core = me % 2
    partner = (dp, me + 1 - 2 * core)
    barrier = pltpu.get_barrier_semaphore()
    pl.semaphore_signal(barrier, inc=1, device_id=partner, device_id_type=MESH_ID)

    def greet(step, carry):
        target = (chip + step) % chips
        pl.semaphore_signal(
            barrier, inc=1, device_id=(dp, target * 2 + core), device_id_type=MESH_ID
        )
        return carry

    lax.fori_loop(1, chips, greet, 0)
    loads = [
        pltpu.make_async_copy(cot_ref, cot, load_sem.at[0]),
        pltpu.make_async_copy(w_ref, weight_out, load_sem.at[1]),
    ]
    for load in loads:
        load.start()

    def chip_copy(step, src, dst, send, recv):
        target = (chip + step) % chips
        return pltpu.make_async_remote_copy(
            src_ref=src(target), dst_ref=dst,
            send_sem=send.at[step], recv_sem=recv.at[step],
            device_id=(dp, target * 2 + core), device_id_type=MESH_ID,
        )

    def send_pairs(step):
        return chip_copy(step, lambda t: msg.at[0, t], inbox.at[0, chip], send0, recv0)

    def send_rows(step):
        return chip_copy(step, lambda t: msg.at[1, t], inbox.at[1, chip], send1, recv1)

    def send_back(step):
        return chip_copy(step, lambda t: back.at[t], back_out.at[chip], send2, recv2)

    def send_keys(step):
        return chip_copy(step, lambda t: key_half.at[t], key_out.at[chip], send3, recv3)

    lane = lax.broadcasted_iota(jnp.int32, (ROWS, 128), 1)
    blank = jnp.zeros((16, SEG), BF16)
    ones = one_rows()
    bias = bias_rows(valid_ref[...])
    batch = 4

    def rows(ref, offset, head):
        return ref[pl.ds(pl.multiple_of((offset + head) * HEAD_DIM, 16), HEAD_DIM)]

    def key_side(head):
        return jnp.concatenate(
            [rows(proj_ref, HEADS, head), rows(proj_ref, 2 * HEADS, head), bias, blank], axis=0
        )

    def pair_batch(at, carry):
        heads = [(chip + at * batch + i) % chips for i in range(batch)]
        packed = [dot(row_select(h), key_side(h), 1, 1).astype(BF16) for h in heads]
        for h, p in zip(heads, packed):
            msg[0, h] = p
        return carry

    lax.fori_loop(0, chips // batch, pair_batch, 0)
    pl.semaphore_wait(barrier, chips)

    def start_pairs(step, carry):
        send_pairs(step).start()
        return carry

    lax.fori_loop(1, chips, start_pairs, 0)
    inbox[0, chip] = msg[0, chip]
    for load in loads:
        load.wait()
    for at in range(0, D, 256):
        grad_ref[at:at + 256] = (
            dot(weight_out[at:at + 256], cot[...], 1, 1) * valid_ref[...]
        ).astype(BF16)

    def end_pairs(step, carry):
        send_pairs(step).wait()
        return carry

    lax.fori_loop(1, chips, end_pairs, 0)

    def pair_copy(at, src, dst):
        return pltpu.make_async_remote_copy(
            src_ref=src, dst_ref=dst, send_sem=pair_send.at[at], recv_sem=pair_recv.at[at],
            device_id=partner, device_id_type=MESH_ID,
        )

    forward = pair_copy(0, inbox.at[0], forwarded)
    forward.start()

    def select_batch(at, carry):
        steps = [at * batch + i for i in range(batch)]
        heads = [(chip + step) % chips for step in steps]
        key_sides = [key_side(h) for h in heads]
        queries = [
            dot(
                row_select(h),
                jnp.concatenate([rows(proj_ref, 0, h), rows(grad_ref, 0, h), ones, blank], axis=0),
                1, 1,
            )
            for h in heads
        ]
        both = [
            jnp.concatenate(
                [
                    jnp.where((lane < 48) | (lane == 96), q, 0.0).astype(BF16),
                    jnp.where((lane >= 48) & (lane < 96), q, 0.0).astype(BF16),
                ],
                axis=0,
            )
            for q in queries
        ]
        scored = [dot(b, side, 1, 0) for b, side in zip(both, key_sides)]
        tops = [jnp.max(r[:ROWS], axis=1, keepdims=True) for r in scored]
        weights = [jnp.exp2(r[:ROWS] * SCALE2 - top * SCALE2) for r, top in zip(scored, tops)]
        totals = [jnp.sum(w, axis=1, keepdims=True) for w in weights]
        deltas = [jnp.sum(w * r[ROWS:], axis=1, keepdims=True) for w, r in zip(weights, scored)]
        for h, q, top, total, delta in zip(heads, queries, tops, totals, deltas):
            place = 97
            for value in (top * SCALE, total, delta):
                for part in three_parts(value):
                    q = jnp.where(lane == place, part, q)
                    place += 1
            msg[1, h] = q.astype(BF16)
        for step in steps:

            @pl.when(step > 0)
            def _(step=step):
                send_rows(step).start()

        return carry

    lax.fori_loop(0, chips // batch, select_batch, 0)
    inbox[1, chip] = msg[1, chip]

    def end_rows(step, carry):
        send_rows(step).wait()
        return carry

    lax.fori_loop(1, chips, end_rows, 0)
    half_keys = chips * ROWS
    queries_in = inbox[1].reshape(half_keys, 128)
    kv_own = inbox[0].reshape(half_keys, 128)
    forward.wait()
    kv = jnp.concatenate([kv_own, forwarded[...].reshape(half_keys, 128)], axis=0)
    chunk = 512
    q_lane = lax.broadcasted_iota(jnp.int32, (chunk, 128), 1)
    row = lax.broadcasted_iota(jnp.int32, (128, chunk), 0)
    key_lane = lax.broadcasted_iota(jnp.int32, (2 * half_keys, 128), 1)

    def front(at):
        qg = queries_in[at:at + chunk]
        zero = jnp.zeros_like(qg)
        query = jnp.where((q_lane < 48) | (q_lane == 96), qg, zero)
        grad = jnp.where((q_lane >= 48) & (q_lane < 96), qg, zero)
        scores = dot(kv, query, 1, 1)
        raw_max = jnp.max(scores, axis=0, keepdims=True)
        weight = jnp.exp2(scores * SCALE2 - raw_max * SCALE2)
        return raw_max, weight, jnp.sum(weight, axis=0, keepdims=True), dot(kv, grad, 1, 1)

    cuts = list(range(0, half_keys, chunk))
    ready = front(cuts[0])
    for n, at in enumerate(cuts):
        raw_max, weight, glob_sum, dprob = ready
        if n + 1 < len(cuts):
            ready = front(cuts[n + 1])
        qg = queries_in[at:at + chunk]
        flipped = qg.astype(F32).T
        loc_max = flipped[97:98] + flipped[98:99] + flipped[99:100]
        loc_sum = flipped[100:101] + flipped[101:102] + flipped[102:103]
        loc_delta = flipped[103:104] + flipped[104:105] + flipped[105:106]
        glob_max = raw_max * SCALE
        top = jnp.maximum(glob_max, loc_max)
        log_total = top + jnp.log(
            loc_sum * jnp.exp(loc_max - top) + glob_sum * jnp.exp(glob_max - top)
        )
        probs = weight * jnp.exp(glob_max - log_total)
        half = probs.astype(BF16)
        out = dot(kv, half, 0, 0)
        delta = jnp.sum(out[48:96] * flipped[48:96], axis=0, keepdims=True)
        delta = delta + loc_delta * jnp.exp(loc_max - log_total)
        dscore = (probs * (dprob - delta)).astype(BF16)
        grad_q = dot(kv, dscore, 0, 0)
        hi, mid, low = three_parts(log_total)
        answer = jnp.where(row < 48, grad_q, jnp.where(row < 96, out, 0.0))
        answer = jnp.where(
            row == 96, hi, jnp.where(row == 97, mid, jnp.where(row == 98, low, answer))
        )
        back[at // ROWS:(at + chunk) // ROWS] = (
            answer.T.astype(BF16).reshape(chunk // ROWS, ROWS, 128)
        )
        term = jnp.where(
            key_lane < 48, dot(dscore, qg, 1, 0),
            jnp.where(key_lane < 96, dot(half, qg, 1, 0), 0.0),
        ).reshape(2, half_keys, 128)
        if n == 0:
            acc[...] = term
        else:
            acc[...] += term

    share = pair_copy(1, acc.at[1], partial)
    share.start()

    def start_back(step, carry):
        send_back(step).start()
        return carry

    lax.fori_loop(1, chips, start_back, 0)
    back_out[chip] = back[chip]
    share.wait()
    key_half[...] = (acc[0] + partial[...]).astype(BF16).reshape(chips, ROWS, 128)

    def start_keys(step, carry):
        send_keys(step).start()
        return carry

    lax.fori_loop(1, chips, start_keys, 0)
    key_out[chip] = key_half[chip]

    def end_back(step, carry):
        send_back(step).wait()
        send_keys(step).wait()
        return carry

    lax.fori_loop(1, chips, end_back, 0)


def dilated_level(projected, cot_rows, w_out, valid):
    packed = jax.ShapeDtypeStruct((HEADS, ROWS, 128), BF16)
    half_keys = HEADS * ROWS
    semaphores = pltpu.SemaphoreType.DMA((HEADS,))
    return pl.pallas_call(
        dilated_body,
        out_shape=(packed, packed, jax.ShapeDtypeStruct((D, SEG), BF16)),
        in_specs=[pl.BlockSpec(memory_space=m) for m in (pltpu.VMEM, pl.ANY, pl.ANY, pltpu.VMEM)],
        out_specs=[pl.BlockSpec(memory_space=pltpu.VMEM)] * 3,
        scratch_shapes=[
            pltpu.VMEM((SEG, D), BF16),
            pltpu.VMEM((D, D), BF16),
            pltpu.SemaphoreType.DMA((2,)),
            pltpu.VMEM((2, HEADS, ROWS, 128), BF16),
            pltpu.VMEM((2, HEADS, ROWS, 128), BF16),
            pltpu.VMEM((HEADS, ROWS, 128), BF16),
            pltpu.VMEM((2, half_keys, 128), F32),
            pltpu.VMEM((half_keys, 128), F32),
            pltpu.VMEM((HEADS, ROWS, 128), BF16),
            pltpu.VMEM((HEADS, ROWS, 128), BF16),
        ] + [semaphores] * 8 + [pltpu.SemaphoreType.DMA((2,))] * 2,
        compiler_params=pltpu.CompilerParams(
            collective_id=0, has_side_effects=True, vmem_limit_bytes=VMEM_LIMIT
        ),
    )(projected, cot_rows, w_out, valid)


def finish_body(total_ref, last_ref, qkv_ref, out_ref):
    qkv_ref[...] = total_ref[:, 0].reshape(D, 256).astype(F32).T

    @pl.when(pl.program_id(0) == 0)
    def _():
        out_ref[...] = last_ref[:, 0].reshape(D, 256).astype(F32)


def finish(total):
    def out_column(i, j):
        return jnp.where(i == 0, j, 2)

    return pl.pallas_call(
        finish_body,
        grid=(3, 3),
        in_specs=[
            pl.BlockSpec((GROUPS, 1, GROUP_ROWS, 256), lambda i, j: (0, i, 0, j)),
            pl.BlockSpec((GROUPS, 1, GROUP_ROWS, 256), lambda i, j: (0, 3, 0, out_column(i, j))),
        ],
        out_specs=[
            pl.BlockSpec((256, D), lambda i, j: (j, i)),
            pl.BlockSpec((D, 256), lambda i, j: (0, out_column(i, j))),
        ],
        out_shape=[jax.ShapeDtypeStruct((D, 3 * D), F32), jax.ShapeDtypeStruct((D, D), F32)],
        compiler_params=pltpu.CompilerParams(vmem_limit_bytes=VMEM_LIMIT),
    )(total, total)


GROUPS = 4
GROUP_HEADS = HEADS // GROUPS
GROUP_ROWS = GROUP_HEADS * HEAD_DIM
PART = GROUP_ROWS // 3
LOCAL_CHUNK = 512


def local_head(head, q_ref, k_ref, v_ref, g_ref, valid_ref, back_ref, key_ref):
    queries, keys, values, grads = q_ref[...], k_ref[...], v_ref[...], g_ref[...]
    keys_more = jnp.concatenate([keys, bias_rows(valid_ref[...])], axis=0)
    queries_more = jnp.concatenate([queries, one_rows()], axis=0)
    select = row_select(head)
    placed = dot(back_ref[0], select, 0, 0)
    key_placed = dot(key_ref[0], select, 0, 0)
    known = placed[96:97] + placed[97:98] + placed[98:99]
    sparse = lax.broadcasted_iota(jnp.int32, (1, LOCAL_CHUNK), 1) % RATE == head

    def front(at):
        cut = slice(at, at + LOCAL_CHUNK)
        scores = dot(keys_more, queries_more[:, cut], 0, 0)
        top = jnp.max(scores, axis=0, keepdims=True)
        weight = jnp.exp2(scores * SCALE2 - top * SCALE2)
        total = jnp.sum(weight, axis=0, keepdims=True)
        return top, weight, total, dot(values, grads[:, cut], 0, 0)

    cuts = list(range(0, SEG, LOCAL_CHUNK))
    context, grad_q = [], []
    grad_k = grad_v = 0.0
    ready = front(cuts[0])
    for n, at in enumerate(cuts):
        top, weight, total, dprob = ready
        if n + 1 < len(cuts):
            ready = front(cuts[n + 1])
        cut = slice(at, at + LOCAL_CHUNK)
        factor = jnp.where(sparse, jnp.exp(top * SCALE - known[:, cut]), 1.0 / total)
        probs = weight * factor
        half = probs.astype(BF16)
        out = dot(values, half, 1, 0) + placed[48:96, cut]
        grad = grads[:, cut]
        delta = jnp.sum(grad.astype(F32) * out, axis=0, keepdims=True)
        context.append((out * valid_ref[:, cut]).astype(BF16))
        dscore = (probs * (dprob - delta)).astype(BF16)
        grad_q.append(((dot(keys, dscore, 1, 0) + placed[0:48, cut]) * SCALE).astype(BF16))
        grad_k = grad_k + dot(dscore, queries[:, cut], 1, 1)
        grad_v = grad_v + dot(half, grad, 1, 1)
    grad_k = ((grad_k.T + key_placed[0:48]) * SCALE).astype(BF16)
    grad_v = (grad_v.T + key_placed[48:96]).astype(BF16)
    return (
        jnp.concatenate(context, axis=1), jnp.concatenate(grad_q, axis=1), grad_k, grad_v
    )


def local_body(
    q_ref, k_ref, v_ref, g_ref, valid_ref, back_ref, key_ref, tok_hbm, cot_hbm, w_hbm,
    att_ref, total_ref,
    tok_ref, cot_ref, w_ref, load_sem, rows_in, ctx, x, pair, got1, sum1, got2, got3, total,
    out_sem, pair_send, pair_recv, send, recv,
):
    head = pl.program_id(0)
    me = lax.axis_index("seq")
    z = lax.axis_index("dp")
    core = me % 2
    where = (me // 8, (me // 2) % 4, z)
    partner = (z, me + 1 - 2 * core)
    axes = [(0, 1, 2), (1, 2, 0), (2, 0, 1)]
    first = [where[axes[p][0]] for p in range(3)]
    second = [where[axes[p][1]] for p in range(3)]
    third = [where[axes[p][2]] for p in range(3)]
    parts, steps = range(3), (2, 1, 3)

    def peer(axis, coordinate):
        px, py, pz = [coordinate if axis == i else where[i] for i in range(3)]
        return (pz, (px * 4 + py) * 2 + core)

    def span(start, size, unit):
        return pl.ds(pl.multiple_of(start, unit), size)

    barrier = pltpu.get_barrier_semaphore()
    loads = [
        pltpu.make_async_copy(src, dst, load_sem.at[i])
        for i, (src, dst) in enumerate(((tok_hbm, tok_ref), (cot_hbm, cot_ref), (w_hbm, w_ref)))
    ]

    @pl.when(head == 0)
    def _():
        for load in loads:
            load.start()
        pl.semaphore_signal(barrier, inc=1, device_id=partner, device_id_type=MESH_ID)
        for axis in range(3):
            for step in range(1, 4):
                pl.semaphore_signal(
                    barrier, inc=1, device_id=peer(axis, (where[axis] + step) % 4), device_id_type=MESH_ID
                )

    @pl.when(head == GROUP_HEADS - 1)
    def _():
        for load in loads:
            load.wait()
        pl.semaphore_wait(barrier, 10)

    def remote(g, part, phase, step, src, dst):
        axis = axes[part][(0, 1, 2, 1, 0)[phase]]
        return pltpu.make_async_remote_copy(
            src_ref=src, dst_ref=dst,
            send_sem=send.at[g, part, phase, step - 1], recv_sem=recv.at[g, part, phase, step - 1],
            device_id=peer(axis, (where[axis] + step) % 4), device_id_type=MESH_ID,
        )

    def pair_out(g):
        return pltpu.make_async_remote_copy(
            src_ref=x.at[g, pl.ds(2 * (1 - core), 2)], dst_ref=pair.at[g],
            send_sem=pair_send.at[g, 0], recv_sem=pair_recv.at[g, 0],
            device_id=partner, device_id_type=MESH_ID,
        )

    def pair_back(g, part, arriving):
        half = pl.ds(2 * ((1 - core) if arriving else core), 2)
        block = total.at[g, half, pl.ds(part * PART, PART)]
        return pltpu.make_async_remote_copy(
            src_ref=block, dst_ref=block,
            send_sem=pair_send.at[g, 1 + part], recv_sem=pair_recv.at[g, 1 + part],
            device_id=partner, device_id_type=MESH_ID,
        )

    def quarter1(part, a):
        return 2 * core + a // 2, span(part * PART + (a % 2) * 32, 32, 32)

    def quarter2(b):
        return span((b // 2) * 16, 16, 16), span((b % 2) * 384, 384, 128)

    def shard(part, b):
        array, _ = quarter1(part, first[part])
        return (
            array,
            span(part * PART + (first[part] % 2) * 32 + (b // 2) * 16, 16, 16),
            span((b % 2) * 384, 384, 128),
        )

    def phase1(g, part, step):
        array, rows = quarter1(part, (first[part] + step) % 4)
        return remote(g, part, 0, step, x.at[g, array, rows], got1.at[g, part, step - 1])

    def phase2(g, part, step):
        rows, cols = quarter2((second[part] + step) % 4)
        return remote(g, part, 1, step, sum1.at[g, part, rows, cols], got2.at[g, part, step - 1])

    def phase3(g, part, step, arriving=False):
        slot = got3.at[g, part, (third[part] + (4 - step if arriving else 0)) % 4]
        return remote(g, part, 2, step, slot, slot)

    def phase4(g, part, step, arriving=False):
        array, rows, cols = shard(part, (second[part] + (4 - step if arriving else 0)) % 4)
        block = total.at[g, array, rows, cols]
        return remote(g, part, 3, step, block, block)

    def phase5(g, part, step, arriving=False):
        array, rows = quarter1(part, (first[part] + (4 - step if arriving else 0)) % 4)
        block = total.at[g, array, rows]
        return remote(g, part, 4, step, block, block)

    def write_back(g):
        return pltpu.make_async_copy(total.at[g], total_ref.at[g], out_sem.at[g])

    def stage1(g):
        pair_out(g).wait_recv()
        for i in range(2):
            x[g, 2 * core + i] = x[g, 2 * core + i] + pair[g, i]
        for part in parts:
            for step in steps:
                phase1(g, part, step).start()
        pair_out(g).wait_send()

    def stage2(g):
        for part in parts:
            for step in steps:
                phase1(g, part, step).wait_recv()
            array, rows = quarter1(part, first[part])
            sum1[g, part] = x[g, array, rows] + got1[g, part, 0] + got1[g, part, 1] + got1[g, part, 2]
            for step in steps:
                phase2(g, part, step).start()
        for part in parts:
            for step in steps:
                phase1(g, part, step).wait_send()

    def stage3(g):
        for part in parts:
            for step in steps:
                phase2(g, part, step).wait_recv()
            rows, cols = quarter2(second[part])
            got3[g, part, third[part]] = (
                sum1[g, part, rows, cols] + got2[g, part, 0] + got2[g, part, 1] + got2[g, part, 2]
            )
            for step in steps:
                phase3(g, part, step).start()
        for part in parts:
            for step in steps:
                phase2(g, part, step).wait_send()

    def stage4(g):
        for part in parts:
            for step in steps:
                phase3(g, part, step, True).wait_recv()
            array, rows, cols = shard(part, second[part])
            total[g, array, rows, cols] = (
                got3[g, part, 0] + got3[g, part, 1] + got3[g, part, 2] + got3[g, part, 3]
            ).astype(BF16)
            for step in steps:
                phase4(g, part, step).start()
        for part in parts:
            for step in steps:
                phase3(g, part, step).wait_send()

    def stage5(g):
        for part in parts:
            for step in steps:
                phase4(g, part, step, True).wait_recv()
            for step in steps:
                phase5(g, part, step).start()
        for part in parts:
            for step in steps:
                phase4(g, part, step).wait_send()

    def stage6(g):
        for part in parts:
            for step in steps:
                phase5(g, part, step, True).wait_recv()
            pair_back(g, part, False).start()
        for part in parts:
            for step in steps:
                phase5(g, part, step).wait_send()

    def stage7(g):
        for part in parts:
            pair_back(g, part, True).wait_recv()
        write_back(g).start()
        for part in parts:
            pair_back(g, part, False).wait_send()

    stages = (stage1, stage2, stage3, stage4, stage5, stage6, stage7)

    context, grad_q, grad_k, grad_v = local_head(
        head, q_ref, k_ref, v_ref, g_ref, valid_ref, back_ref, key_ref
    )
    here = span((head % GROUP_HEADS) * HEAD_DIM, HEAD_DIM, 16)
    rows_in[0, here] = grad_q
    rows_in[1, here] = grad_k
    rows_in[2, here] = grad_v
    rows_in[3, here] = context
    ctx[span(head * HEAD_DIM, HEAD_DIM, 16)] = context

    @pl.when(head % GROUP_HEADS == GROUP_HEADS - 1)
    def _():
        g = head // GROUP_HEADS

        def products(arrays):
            for i in arrays:
                x[g, i] = dot(rows_in[i], (cot_ref if i == 3 else tok_ref)[...], 1, 0)

        @pl.when(core == 0)
        def _():
            products((2, 3))

        @pl.when(core == 1)
        def _():
            products((0, 1))

        pair_out(g).start()

        @pl.when(core == 0)
        def _():
            products((0, 1))

        @pl.when(core == 1)
        def _():
            products((2, 3))

    for k, stage in enumerate(stages, 1):
        since = head - (GROUP_HEADS - 1) - k

        @pl.when((since >= 0) & (since % GROUP_HEADS == 0))
        def _(stage=stage, since=since):
            stage(since // GROUP_HEADS)

    @pl.when(head == HEADS - 1)
    def _():
        stage1(3)
        stage5(2)
        att_ref[...] = dot(ctx[...], w_ref[...], 0, 0).astype(BF16)
        stage2(3)
        stage6(2)
        stage3(3)
        stage7(2)
        stage4(3)
        stage5(3)
        stage6(3)
        stage7(3)
        for g in range(GROUPS):
            write_back(g).wait()


def shards(tokens, cotangent, lengths, w_qkv, w_out):
    token_rows = tokens[0]
    cot_rows = cotangent[0]
    first_pos = lax.axis_index("seq") * SEG
    row_valid = first_pos + jnp.arange(SEG, dtype=jnp.int32) < lengths[0]
    valid = row_valid.astype(F32)[None, :]
    projected = dot(w_qkv, token_rows, 0, 1).astype(BF16)
    back_own, key_own, grad_ctx = dilated_level(projected, cot_rows, w_out, valid)

    def head_block(offset):
        return pl.BlockSpec((HEAD_DIM, SEG), lambda h: (h + offset, 0))

    head_specs = [head_block(0), head_block(HEADS), head_block(2 * HEADS), head_block(0)]
    heads = (projected, projected, projected, grad_ctx)
    packed = pl.BlockSpec((1, ROWS, 128), lambda h: (h, 0, 0))
    def whole(*shape):
        return pl.BlockSpec(shape, lambda h: (0,) * len(shape), pipeline_mode=pl.Buffered(1))

    attended, total = pl.pallas_call(
        local_body,
        grid=(HEADS,),
        in_specs=head_specs + [
            whole(1, SEG),
            packed,
            packed,
        ] + [pl.BlockSpec(memory_space=pl.ANY)] * 3,
        out_specs=[whole(SEG, D), pl.BlockSpec(memory_space=pl.ANY)],
        out_shape=[
            jax.ShapeDtypeStruct((SEG, D), BF16),
            jax.ShapeDtypeStruct((GROUPS, 4, GROUP_ROWS, D), BF16),
        ],
        scratch_shapes=[
            pltpu.VMEM((SEG, D), BF16),
            pltpu.VMEM((SEG, D), BF16),
            pltpu.VMEM((D, D), BF16),
            pltpu.SemaphoreType.DMA((3,)),
            pltpu.VMEM((4, GROUP_ROWS, SEG), BF16),
            pltpu.VMEM((D, SEG), BF16),
            pltpu.VMEM((GROUPS, 4, GROUP_ROWS, D), F32),
            pltpu.VMEM((GROUPS, 2, GROUP_ROWS, D), F32),
            pltpu.VMEM((GROUPS, 3, 3, 32, D), F32),
            pltpu.VMEM((GROUPS, 3, 32, D), F32),
            pltpu.VMEM((GROUPS, 3, 3, 16, 384), F32),
            pltpu.VMEM((GROUPS, 3, 4, 16, 384), F32),
            pltpu.VMEM((GROUPS, 4, GROUP_ROWS, D), BF16),
            pltpu.SemaphoreType.DMA((GROUPS,)),
            pltpu.SemaphoreType.DMA((GROUPS, 4)),
            pltpu.SemaphoreType.DMA((GROUPS, 4)),
            pltpu.SemaphoreType.DMA((GROUPS, 3, 5, 3)),
            pltpu.SemaphoreType.DMA((GROUPS, 3, 5, 3)),
        ],
        compiler_params=pltpu.CompilerParams(
            collective_id=2, has_side_effects=True, vmem_limit_bytes=60 * 2**20
        ),
    )(*heads, valid, back_own, key_own, token_rows, cot_rows, w_out)

    grad_qkv, grad_out = finish(total)
    return attended[None], grad_qkv, grad_out


def solution(mesh):
    return jax.shard_map(
        shards,
        mesh=mesh,
        in_specs=(P("dp", "seq", None), P("dp", "seq", None), P("dp"), P(), P()),
        out_specs=(P("dp", "seq", None), P(), P()),
        check_vma=False,
    )
```

```python
import math

import jax
import jax.numpy as jnp
from jax import lax
from jax.experimental import pallas as pl
from jax.experimental.pallas import tpu as pltpu
from jax.sharding import PartitionSpec as P

D = 768
HEADS = 16
HEAD_DIM = 48
SEG = 1024
RATE = 16
ROWS = SEG // RATE
SCALE = HEAD_DIM ** -0.5
SCALE2 = SCALE * math.log2(math.e)
MASKED = -1e30
MESH_ID = pl.DeviceIdType.MESH
F32 = jnp.float32
BF16 = jnp.bfloat16
VMEM_LIMIT = 56 * 2**20


def dot(left, right, left_dim, right_dim):
    return lax.dot_general(
        left, right, (((left_dim,), (right_dim,)), ((), ())), preferred_element_type=F32
    )


def three_parts(x):
    hi = x.astype(BF16).astype(F32)
    rest = x - hi
    mid = rest.astype(BF16).astype(F32)
    return hi, mid, (rest - mid).astype(BF16).astype(F32)


def row_select(head):
    row = lax.broadcasted_iota(jnp.int32, (ROWS, SEG), 0)
    col = lax.broadcasted_iota(jnp.int32, (ROWS, SEG), 1)
    return jnp.where(col == row * RATE + head, 1.0, 0.0).astype(BF16)


def one_rows():
    row = lax.broadcasted_iota(jnp.int32, (16, SEG), 0)
    return jnp.where(row == 0, 1.0, 0.0).astype(BF16)


def bias_rows(valid):
    row = lax.broadcasted_iota(jnp.int32, (16, SEG), 0)
    return jnp.where(row == 0, (1.0 - valid) * MASKED, 0.0).astype(BF16)


def dilated_body(
    proj_ref, cot_ref, w_ref, valid_ref, back_out, key_out, grad_ref,
    cot, weight_out, load_sem, msg, inbox, forwarded, acc, partial, back, key_half,
    send0, recv0, send1, recv1, send2, recv2, send3, recv3, pair_send, pair_recv,
):
    me = lax.axis_index("seq")
    dp = lax.axis_index("dp")
    chips = HEADS
    chip = me // 2
    core = me % 2
    partner = (dp, me + 1 - 2 * core)
    barrier = pltpu.get_barrier_semaphore()
    pl.semaphore_signal(barrier, inc=1, device_id=partner, device_id_type=MESH_ID)

    def greet(step, carry):
        target = (chip + step) % chips
        pl.semaphore_signal(
            barrier, inc=1, device_id=(dp, target * 2 + core), device_id_type=MESH_ID
        )
        return carry

    lax.fori_loop(1, chips, greet, 0)
    loads = [
        pltpu.make_async_copy(cot_ref, cot, load_sem.at[0]),
        pltpu.make_async_copy(w_ref, weight_out, load_sem.at[1]),
    ]
    for load in loads:
        load.start()

    def chip_copy(step, src, dst, send, recv):
        target = (chip + step) % chips
        return pltpu.make_async_remote_copy(
            src_ref=src(target), dst_ref=dst,
            send_sem=send.at[step], recv_sem=recv.at[step],
            device_id=(dp, target * 2 + core), device_id_type=MESH_ID,
        )

    def send_pairs(step):
        return chip_copy(step, lambda t: msg.at[0, t], inbox.at[0, chip], send0, recv0)

    def send_rows(step):
        return chip_copy(step, lambda t: msg.at[1, t], inbox.at[1, chip], send1, recv1)

    def send_back(step):
        return chip_copy(step, lambda t: back.at[t], back_out.at[chip], send2, recv2)

    def send_keys(step):
        return chip_copy(step, lambda t: key_half.at[t], key_out.at[chip], send3, recv3)

    lane = lax.broadcasted_iota(jnp.int32, (ROWS, 128), 1)
    blank = jnp.zeros((16, SEG), BF16)
    ones = one_rows()
    bias = bias_rows(valid_ref[...])
    batch = 4

    def rows(ref, offset, head):
        return ref[pl.ds(pl.multiple_of((offset + head) * HEAD_DIM, 16), HEAD_DIM)]

    def key_side(head):
        return jnp.concatenate(
            [rows(proj_ref, HEADS, head), rows(proj_ref, 2 * HEADS, head), bias, blank], axis=0
        )

    def pair_batch(at, carry):
        heads = [(chip + at * batch + i) % chips for i in range(batch)]
        packed = [dot(row_select(h), key_side(h), 1, 1).astype(BF16) for h in heads]
        for h, p in zip(heads, packed):
            msg[0, h] = p
        return carry

    lax.fori_loop(0, chips // batch, pair_batch, 0)
    pl.semaphore_wait(barrier, chips)

    def start_pairs(step, carry):
        send_pairs(step).start()
        return carry

    lax.fori_loop(1, chips, start_pairs, 0)
    inbox[0, chip] = msg[0, chip]
    for load in loads:
        load.wait()
    for at in range(0, D, 256):
        grad_ref[at:at + 256] = (
            dot(weight_out[at:at + 256], cot[...], 1, 1) * valid_ref[...]
        ).astype(BF16)

    def end_pairs(step, carry):
        send_pairs(step).wait()
        return carry

    lax.fori_loop(1, chips, end_pairs, 0)

    def pair_copy(at, src, dst):
        return pltpu.make_async_remote_copy(
            src_ref=src, dst_ref=dst, send_sem=pair_send.at[at], recv_sem=pair_recv.at[at],
            device_id=partner, device_id_type=MESH_ID,
        )

    forward = pair_copy(0, inbox.at[0], forwarded)
    forward.start()

    def select_batch(at, carry):
        steps = [at * batch + i for i in range(batch)]
        heads = [(chip + step) % chips for step in steps]
        key_sides = [key_side(h) for h in heads]
        queries = [
            dot(
                row_select(h),
                jnp.concatenate([rows(proj_ref, 0, h), rows(grad_ref, 0, h), ones, blank], axis=0),
                1, 1,
            )
            for h in heads
        ]
        both = [
            jnp.concatenate(
                [
                    jnp.where((lane < 48) | (lane == 96), q, 0.0).astype(BF16),
                    jnp.where((lane >= 48) & (lane < 96), q, 0.0).astype(BF16),
                ],
                axis=0,
            )
            for q in queries
        ]
        scored = [dot(b, side, 1, 0) for b, side in zip(both, key_sides)]
        tops = [jnp.max(r[:ROWS], axis=1, keepdims=True) for r in scored]
        weights = [jnp.exp2(r[:ROWS] * SCALE2 - top * SCALE2) for r, top in zip(scored, tops)]
        totals = [jnp.sum(w, axis=1, keepdims=True) for w in weights]
        deltas = [jnp.sum(w * r[ROWS:], axis=1, keepdims=True) for w, r in zip(weights, scored)]
        for h, q, top, total, delta in zip(heads, queries, tops, totals, deltas):
            place = 97
            for value in (top * SCALE, total, delta):
                for part in three_parts(value):
                    q = jnp.where(lane == place, part, q)
                    place += 1
            msg[1, h] = q.astype(BF16)
        for step in steps:

            @pl.when(step > 0)
            def _(step=step):
                send_rows(step).start()

        return carry

    lax.fori_loop(0, chips // batch, select_batch, 0)
    inbox[1, chip] = msg[1, chip]

    def end_rows(step, carry):
        send_rows(step).wait()
        return carry

    lax.fori_loop(1, chips, end_rows, 0)
    half_keys = chips * ROWS
    queries_in = inbox[1].reshape(half_keys, 128)
    kv_own = inbox[0].reshape(half_keys, 128)
    forward.wait()
    kv = jnp.concatenate([kv_own, forwarded[...].reshape(half_keys, 128)], axis=0)
    chunk = 512
    q_lane = lax.broadcasted_iota(jnp.int32, (chunk, 128), 1)
    row = lax.broadcasted_iota(jnp.int32, (128, chunk), 0)
    key_lane = lax.broadcasted_iota(jnp.int32, (half_keys, 128), 1)

    def front(at):
        qg = queries_in[at:at + chunk]
        zero = jnp.zeros_like(qg)
        query = jnp.where((q_lane < 48) | (q_lane == 96), qg, zero)
        grad = jnp.where((q_lane >= 48) & (q_lane < 96), qg, zero)
        scores = dot(kv, query, 1, 1)
        raw_max = jnp.max(scores, axis=0, keepdims=True)
        weight = jnp.exp2(scores * SCALE2 - raw_max * SCALE2)
        return raw_max, weight, jnp.sum(weight, axis=0, keepdims=True), dot(kv, grad, 1, 1)

    def share(piece):
        span = pl.ds(piece * (half_keys // 4), half_keys // 4)
        return pair_copy(1 + piece, acc.at[1, span], partial.at[span])

    def start_range(copy, base, size):
        def start_one(i, carry):
            step = (base + (i + chip) % size - chip + chips) % chips

            @pl.when(step > 0)
            def _():
                copy(step).start()

            return carry

        lax.fori_loop(0, size, start_one, 0)

    cuts = list(range(0, half_keys, chunk))
    ready = front(cuts[0])
    for n, at in enumerate(cuts):
        raw_max, weight, glob_sum, dprob = ready
        if n + 1 < len(cuts):
            ready = front(cuts[n + 1])
        qg = queries_in[at:at + chunk]
        flipped = qg.astype(F32).T
        loc_max = flipped[97:98] + flipped[98:99] + flipped[99:100]
        loc_sum = flipped[100:101] + flipped[101:102] + flipped[102:103]
        loc_delta = flipped[103:104] + flipped[104:105] + flipped[105:106]
        glob_max = raw_max * SCALE
        top = jnp.maximum(glob_max, loc_max)
        log_total = top + jnp.log(
            loc_sum * jnp.exp(loc_max - top) + glob_sum * jnp.exp(glob_max - top)
        )
        probs = weight * jnp.exp(glob_max - log_total)
        half = probs.astype(BF16)
        out = dot(kv, half, 0, 0)
        delta = jnp.sum(out[48:96] * flipped[48:96], axis=0, keepdims=True)
        delta = delta + loc_delta * jnp.exp(loc_max - log_total)
        dscore = (probs * (dprob - delta)).astype(BF16)
        grad_q = dot(kv, dscore, 0, 0)
        hi, mid, low = three_parts(log_total)
        answer = jnp.where(row < 48, grad_q, jnp.where(row < 96, out, 0.0))
        answer = jnp.where(
            row == 96, hi, jnp.where(row == 97, mid, jnp.where(row == 98, low, answer))
        )
        back[at // ROWS:(at + chunk) // ROWS] = (
            answer.T.astype(BF16).reshape(chunk // ROWS, ROWS, 128)
        )
        start_range(send_back, at // ROWS, chunk // ROWS)
        for slot in (1, 0):
            span = slice(slot * half_keys, (slot + 1) * half_keys)
            term = jnp.where(
                key_lane < 48, dot(dscore[span], qg, 1, 0),
                jnp.where(key_lane < 96, dot(half[span], qg, 1, 0), 0.0),
            )
            if n == 0:
                acc[slot] = term
            else:
                acc[slot] += term
            if slot == 1 and n + 1 == len(cuts):
                for piece in range(4):
                    share(piece).start()

    back_out[chip] = back[chip]
    for piece in range(4):
        share(piece).wait()
        span = slice(piece * (half_keys // 4), (piece + 1) * (half_keys // 4))
        key_half[piece * 4:piece * 4 + 4] = (
            (acc[0, span] + partial[span]).astype(BF16).reshape(4, ROWS, 128)
        )
        start_range(send_keys, piece * 4, 4)
    key_out[chip] = key_half[chip]

    def end_back(step, carry):
        send_back(step).wait()
        send_keys(step).wait()
        return carry

    lax.fori_loop(1, chips, end_back, 0)


def dilated_level(projected, cot_rows, w_out, valid):
    packed = jax.ShapeDtypeStruct((HEADS, ROWS, 128), BF16)
    half_keys = HEADS * ROWS
    semaphores = pltpu.SemaphoreType.DMA((HEADS,))
    return pl.pallas_call(
        dilated_body,
        out_shape=(packed, packed, jax.ShapeDtypeStruct((D, SEG), BF16)),
        in_specs=[pl.BlockSpec(memory_space=m) for m in (pltpu.VMEM, pl.ANY, pl.ANY, pltpu.VMEM)],
        out_specs=[pl.BlockSpec(memory_space=pltpu.VMEM)] * 3,
        scratch_shapes=[
            pltpu.VMEM((SEG, D), BF16),
            pltpu.VMEM((D, D), BF16),
            pltpu.SemaphoreType.DMA((2,)),
            pltpu.VMEM((2, HEADS, ROWS, 128), BF16),
            pltpu.VMEM((2, HEADS, ROWS, 128), BF16),
            pltpu.VMEM((HEADS, ROWS, 128), BF16),
            pltpu.VMEM((2, half_keys, 128), F32),
            pltpu.VMEM((half_keys, 128), F32),
            pltpu.VMEM((HEADS, ROWS, 128), BF16),
            pltpu.VMEM((HEADS, ROWS, 128), BF16),
        ] + [semaphores] * 8 + [pltpu.SemaphoreType.DMA((5,))] * 2,
        compiler_params=pltpu.CompilerParams(
            collective_id=0, has_side_effects=True, vmem_limit_bytes=VMEM_LIMIT
        ),
    )(projected, cot_rows, w_out, valid)


def finish_body(total_ref, last_ref, qkv_ref, out_ref):
    qkv_ref[...] = total_ref[:, 0].reshape(D, D).astype(F32).T

    @pl.when(pl.program_id(0) == 0)
    def _():
        out_ref[...] = last_ref[:, 0].reshape(D, D).astype(F32)


def finish(total):
    return pl.pallas_call(
        finish_body,
        grid=(3,),
        in_specs=[
            pl.BlockSpec((GROUPS, 1, GROUP_ROWS, D), lambda i: (0, i, 0, 0)),
            pl.BlockSpec((GROUPS, 1, GROUP_ROWS, D), lambda i: (0, 3, 0, 0)),
        ],
        out_specs=[pl.BlockSpec((D, D), lambda i: (0, i)), pl.BlockSpec((D, D), lambda i: (0, 0))],
        out_shape=[jax.ShapeDtypeStruct((D, 3 * D), F32), jax.ShapeDtypeStruct((D, D), F32)],
        compiler_params=pltpu.CompilerParams(vmem_limit_bytes=VMEM_LIMIT),
    )(total, total)


GROUPS = 4
GROUP_HEADS = HEADS // GROUPS
GROUP_ROWS = GROUP_HEADS * HEAD_DIM
PART = GROUP_ROWS // 3
LOCAL_CHUNK = 512


def local_head(head, q_ref, k_ref, v_ref, g_ref, valid_ref, back_ref, key_ref):
    queries, keys, values, grads = q_ref[...], k_ref[...], v_ref[...], g_ref[...]
    keys_more = jnp.concatenate([keys, bias_rows(valid_ref[...])], axis=0)
    queries_more = jnp.concatenate([queries, one_rows()], axis=0)
    select = row_select(head)
    placed = dot(back_ref[0], select, 0, 0)
    key_placed = dot(key_ref[0], select, 0, 0)
    known = placed[96:97] + placed[97:98] + placed[98:99]
    sparse = lax.broadcasted_iota(jnp.int32, (1, LOCAL_CHUNK), 1) % RATE == head

    def front(at):
        cut = slice(at, at + LOCAL_CHUNK)
        scores = dot(keys_more, queries_more[:, cut], 0, 0)
        top = jnp.max(scores, axis=0, keepdims=True)
        weight = jnp.exp2(scores * SCALE2 - top * SCALE2)
        total = jnp.sum(weight, axis=0, keepdims=True)
        return top, weight, total, dot(values, grads[:, cut], 0, 0)

    cuts = list(range(0, SEG, LOCAL_CHUNK))
    context, grad_q = [], []
    grad_k = grad_v = 0.0
    ready = front(cuts[0])
    for n, at in enumerate(cuts):
        top, weight, total, dprob = ready
        if n + 1 < len(cuts):
            ready = front(cuts[n + 1])
        cut = slice(at, at + LOCAL_CHUNK)
        factor = jnp.where(sparse, jnp.exp(top * SCALE - known[:, cut]), 1.0 / total)
        probs = weight * factor
        half = probs.astype(BF16)
        out = dot(values, half, 1, 0) + placed[48:96, cut]
        grad = grads[:, cut]
        delta = jnp.sum(grad.astype(F32) * out, axis=0, keepdims=True)
        context.append((out * valid_ref[:, cut]).astype(BF16))
        dscore = (probs * (dprob - delta)).astype(BF16)
        grad_q.append(((dot(keys, dscore, 1, 0) + placed[0:48, cut]) * SCALE).astype(BF16))
        grad_k = grad_k + dot(dscore, queries[:, cut], 1, 1)
        grad_v = grad_v + dot(half, grad, 1, 1)
    grad_k = ((grad_k.T + key_placed[0:48]) * SCALE).astype(BF16)
    grad_v = (grad_v.T + key_placed[48:96]).astype(BF16)
    return (
        jnp.concatenate(context, axis=1), jnp.concatenate(grad_q, axis=1), grad_k, grad_v
    )


def local_body(
    q_ref, k_ref, v_ref, g_ref, valid_ref, back_ref, key_ref, tok_hbm, cot_hbm, w_hbm,
    att_ref, total_ref,
    tok_ref, cot_ref, w_ref, load_sem, rows_in, ctx, x, pair, got1, sum1, got2, got3, total,
    out_sem, pair_send, pair_recv, send, recv,
):
    head = pl.program_id(0)
    me = lax.axis_index("seq")
    z = lax.axis_index("dp")
    core = me % 2
    where = (me // 8, (me // 2) % 4, z)
    partner = (z, me + 1 - 2 * core)
    axes = [(0, 1, 2), (1, 2, 0), (2, 0, 1)]
    first = [where[axes[p][0]] for p in range(3)]
    second = [where[axes[p][1]] for p in range(3)]
    third = [where[axes[p][2]] for p in range(3)]
    parts, steps = range(3), (2, 1, 3)

    def peer(axis, coordinate):
        px, py, pz = [coordinate if axis == i else where[i] for i in range(3)]
        return (pz, (px * 4 + py) * 2 + core)

    def span(start, size, unit):
        return pl.ds(pl.multiple_of(start, unit), size)

    barrier = pltpu.get_barrier_semaphore()
    loads = [
        pltpu.make_async_copy(src, dst, load_sem.at[i])
        for i, (src, dst) in enumerate(((tok_hbm, tok_ref), (cot_hbm, cot_ref), (w_hbm, w_ref)))
    ]

    @pl.when(head == 0)
    def _():
        for load in loads:
            load.start()
        pl.semaphore_signal(barrier, inc=1, device_id=partner, device_id_type=MESH_ID)
        for axis in range(3):
            for step in range(1, 4):
                pl.semaphore_signal(
                    barrier, inc=1, device_id=peer(axis, (where[axis] + step) % 4), device_id_type=MESH_ID
                )

    @pl.when(head == GROUP_HEADS - 1)
    def _():
        for load in loads:
            load.wait()
        pl.semaphore_wait(barrier, 10)

    def remote(g, part, phase, step, src, dst):
        axis = axes[part][(0, 1, 2, 1, 0)[phase]]
        return pltpu.make_async_remote_copy(
            src_ref=src, dst_ref=dst,
            send_sem=send.at[g, part, phase, step - 1], recv_sem=recv.at[g, part, phase, step - 1],
            device_id=peer(axis, (where[axis] + step) % 4), device_id_type=MESH_ID,
        )

    def pair_out(g, part):
        rows = pl.ds(part * PART, PART)
        return pltpu.make_async_remote_copy(
            src_ref=x.at[g, pl.ds(2 * (1 - core), 2), rows], dst_ref=pair.at[g, :, rows],
            send_sem=pair_send.at[g, part], recv_sem=pair_recv.at[g, part],
            device_id=partner, device_id_type=MESH_ID,
        )

    def pair_back(g, part, arriving):
        half = pl.ds(2 * ((1 - core) if arriving else core), 2)
        block = total.at[g, half, pl.ds(part * PART, PART)]
        return pltpu.make_async_remote_copy(
            src_ref=block, dst_ref=block,
            send_sem=pair_send.at[g, 3 + part], recv_sem=pair_recv.at[g, 3 + part],
            device_id=partner, device_id_type=MESH_ID,
        )

    def quarter1(part, a):
        return 2 * core + a // 2, span(part * PART + (a % 2) * 32, 32, 32)

    def quarter2(b):
        return span((b // 2) * 16, 16, 16), span((b % 2) * 384, 384, 128)

    def shard(part, b):
        array, _ = quarter1(part, first[part])
        return (
            array,
            span(part * PART + (first[part] % 2) * 32 + (b // 2) * 16, 16, 16),
            span((b % 2) * 384, 384, 128),
        )

    def phase1(g, part, step):
        array, rows = quarter1(part, (first[part] + step) % 4)
        return remote(g, part, 0, step, x.at[g, array, rows], got1.at[g, part, step - 1])

    def phase2(g, part, step):
        rows, cols = quarter2((second[part] + step) % 4)
        return remote(g, part, 1, step, sum1.at[g, part, rows, cols], got2.at[g, part, step - 1])

    def phase3(g, part, step, arriving=False):
        slot = got3.at[g, part, (third[part] + (4 - step if arriving else 0)) % 4]
        return remote(g, part, 2, step, slot, slot)

    def phase4(g, part, step, arriving=False):
        array, rows, cols = shard(part, (second[part] + (4 - step if arriving else 0)) % 4)
        block = total.at[g, array, rows, cols]
        return remote(g, part, 3, step, block, block)

    def phase5(g, part, step, arriving=False):
        array, rows = quarter1(part, (first[part] + (4 - step if arriving else 0)) % 4)
        block = total.at[g, array, rows]
        return remote(g, part, 4, step, block, block)

    def write_back(g):
        return pltpu.make_async_copy(total.at[g], total_ref.at[g], out_sem.at[g])

    def stage1(g):
        for part in parts:
            pair_out(g, part).wait_recv()
            rows = slice(part * PART, (part + 1) * PART)
            for i in range(2):
                x[g, 2 * core + i, rows] = x[g, 2 * core + i, rows] + pair[g, i, rows]
            for step in steps:
                phase1(g, part, step).start()
        for part in parts:
            pair_out(g, part).wait_send()

    def stage2(g):
        for part in parts:
            for step in steps:
                phase1(g, part, step).wait_recv()
            array, rows = quarter1(part, first[part])
            sum1[g, part] = x[g, array, rows] + got1[g, part, 0] + got1[g, part, 1] + got1[g, part, 2]
            for step in steps:
                phase2(g, part, step).start()
        for part in parts:
            for step in steps:
                phase1(g, part, step).wait_send()

    def stage3(g):
        for part in parts:
            for step in steps:
                phase2(g, part, step).wait_recv()
            rows, cols = quarter2(second[part])
            got3[g, part, third[part]] = (
                sum1[g, part, rows, cols] + got2[g, part, 0] + got2[g, part, 1] + got2[g, part, 2]
            )
            for step in steps:
                phase3(g, part, step).start()
        for part in parts:
            for step in steps:
                phase2(g, part, step).wait_send()

    def stage4(g):
        for part in parts:
            for step in steps:
                phase3(g, part, step, True).wait_recv()
            array, rows, cols = shard(part, second[part])
            total[g, array, rows, cols] = (
                got3[g, part, 0] + got3[g, part, 1] + got3[g, part, 2] + got3[g, part, 3]
            ).astype(BF16)
            for step in steps:
                phase4(g, part, step).start()
        for part in parts:
            for step in steps:
                phase3(g, part, step).wait_send()

    def stage5(g):
        for part in parts:
            for step in steps:
                phase4(g, part, step, True).wait_recv()
            for step in steps:
                phase5(g, part, step).start()
        for part in parts:
            for step in steps:
                phase4(g, part, step).wait_send()

    def stage6(g):
        for part in parts:
            for step in steps:
                phase5(g, part, step, True).wait_recv()
            pair_back(g, part, False).start()
        for part in parts:
            for step in steps:
                phase5(g, part, step).wait_send()

    def stage7(g):
        for part in parts:
            pair_back(g, part, True).wait_recv()
        write_back(g).start()
        for part in parts:
            pair_back(g, part, False).wait_send()

    stages = (stage1, stage2, stage3, stage4, stage5, stage6, stage7)

    context, grad_q, grad_k, grad_v = local_head(
        head, q_ref, k_ref, v_ref, g_ref, valid_ref, back_ref, key_ref
    )
    here = span((head % GROUP_HEADS) * HEAD_DIM, HEAD_DIM, 16)
    rows_in[0, here] = grad_q
    rows_in[1, here] = grad_k
    rows_in[2, here] = grad_v
    rows_in[3, here] = context
    ctx[span(head * HEAD_DIM, HEAD_DIM, 16)] = context

    @pl.when(head % GROUP_HEADS == GROUP_HEADS - 1)
    def _():
        g = head // GROUP_HEADS

        def products(arrays):
            for i in arrays:
                x[g, i] = dot(rows_in[i], (cot_ref if i == 3 else tok_ref)[...], 1, 0)

        @pl.when(core == 0)
        def _():
            products((2, 3))

        @pl.when(core == 1)
        def _():
            products((0, 1))

        for part in parts:
            pair_out(g, part).start()

        @pl.when(core == 0)
        def _():
            products((0, 1))

        @pl.when(core == 1)
        def _():
            products((2, 3))

    for k, stage in enumerate(stages, 1):
        since = head - (GROUP_HEADS - 1) - k

        @pl.when((since >= 0) & (since % GROUP_HEADS == 0))
        def _(stage=stage, since=since):
            stage(since // GROUP_HEADS)

    @pl.when(head == HEADS - 1)
    def _():
        stage1(3)
        stage5(2)
        att_ref[...] = dot(ctx[...], w_ref[...], 0, 0).astype(BF16)
        stage2(3)
        stage6(2)
        stage3(3)
        stage7(2)
        stage4(3)
        stage5(3)
        stage6(3)
        stage7(3)
        for g in range(GROUPS):
            write_back(g).wait()


def shards(tokens, cotangent, lengths, w_qkv, w_out):
    token_rows = tokens[0]
    cot_rows = cotangent[0]
    first_pos = lax.axis_index("seq") * SEG
    row_valid = first_pos + jnp.arange(SEG, dtype=jnp.int32) < lengths[0]
    valid = row_valid.astype(F32)[None, :]
    projected = dot(w_qkv, token_rows, 0, 1).astype(BF16)
    back_own, key_own, grad_ctx = dilated_level(projected, cot_rows, w_out, valid)

    def head_block(offset):
        return pl.BlockSpec((HEAD_DIM, SEG), lambda h: (h + offset, 0))

    head_specs = [head_block(0), head_block(HEADS), head_block(2 * HEADS), head_block(0)]
    heads = (projected, projected, projected, grad_ctx)
    packed = pl.BlockSpec((1, ROWS, 128), lambda h: (h, 0, 0))
    def whole(*shape):
        return pl.BlockSpec(shape, lambda h: (0,) * len(shape), pipeline_mode=pl.Buffered(1))

    attended, total = pl.pallas_call(
        local_body,
        grid=(HEADS,),
        in_specs=head_specs + [
            whole(1, SEG),
            packed,
            packed,
        ] + [pl.BlockSpec(memory_space=pl.ANY)] * 3,
        out_specs=[whole(SEG, D), pl.BlockSpec(memory_space=pl.ANY)],
        out_shape=[
            jax.ShapeDtypeStruct((SEG, D), BF16),
            jax.ShapeDtypeStruct((GROUPS, 4, GROUP_ROWS, D), BF16),
        ],
        scratch_shapes=[
            pltpu.VMEM((SEG, D), BF16),
            pltpu.VMEM((SEG, D), BF16),
            pltpu.VMEM((D, D), BF16),
            pltpu.SemaphoreType.DMA((3,)),
            pltpu.VMEM((4, GROUP_ROWS, SEG), BF16),
            pltpu.VMEM((D, SEG), BF16),
            pltpu.VMEM((GROUPS, 4, GROUP_ROWS, D), F32),
            pltpu.VMEM((GROUPS, 2, GROUP_ROWS, D), F32),
            pltpu.VMEM((GROUPS, 3, 3, 32, D), F32),
            pltpu.VMEM((GROUPS, 3, 32, D), F32),
            pltpu.VMEM((GROUPS, 3, 3, 16, 384), F32),
            pltpu.VMEM((GROUPS, 3, 4, 16, 384), F32),
            pltpu.VMEM((GROUPS, 4, GROUP_ROWS, D), BF16),
            pltpu.SemaphoreType.DMA((GROUPS,)),
            pltpu.SemaphoreType.DMA((GROUPS, 6)),
            pltpu.SemaphoreType.DMA((GROUPS, 6)),
            pltpu.SemaphoreType.DMA((GROUPS, 3, 5, 3)),
            pltpu.SemaphoreType.DMA((GROUPS, 3, 5, 3)),
        ],
        compiler_params=pltpu.CompilerParams(
            collective_id=2, has_side_effects=True, vmem_limit_bytes=60 * 2**20
        ),
    )(*heads, valid, back_own, key_own, token_rows, cot_rows, w_out)

    grad_qkv, grad_out = finish(total)
    return attended[None], grad_qkv, grad_out


def solution(mesh):
    return jax.shard_map(
        shards,
        mesh=mesh,
        in_specs=(P("dp", "seq", None), P("dp", "seq", None), P("dp"), P(), P()),
        out_specs=(P("dp", "seq", None), P(), P()),
        check_vma=False,
    )
```

```python
import math

import jax
import jax.numpy as jnp
from jax import lax
from jax.experimental import pallas as pl
from jax.experimental.pallas import tpu as pltpu
from jax.sharding import PartitionSpec as P

D = 768
HEADS = 16
HEAD_DIM = 48
SEG = 1024
RATE = 16
ROWS = SEG // RATE
SCALE = HEAD_DIM ** -0.5
SCALE2 = SCALE * math.log2(math.e)
MASKED = -1e30
MESH_ID = pl.DeviceIdType.MESH
F32 = jnp.float32
BF16 = jnp.bfloat16
VMEM_LIMIT = 56 * 2**20


def dot(left, right, left_dim, right_dim):
    return lax.dot_general(
        left, right, (((left_dim,), (right_dim,)), ((), ())), preferred_element_type=F32
    )


def three_parts(x):
    hi = x.astype(BF16).astype(F32)
    rest = x - hi
    mid = rest.astype(BF16).astype(F32)
    return hi, mid, (rest - mid).astype(BF16).astype(F32)


def row_select(head):
    row = lax.broadcasted_iota(jnp.int32, (ROWS, SEG), 0)
    col = lax.broadcasted_iota(jnp.int32, (ROWS, SEG), 1)
    return jnp.where(col == row * RATE + head, 1.0, 0.0).astype(BF16)


def one_rows():
    row = lax.broadcasted_iota(jnp.int32, (16, SEG), 0)
    return jnp.where(row == 0, 1.0, 0.0).astype(BF16)


def bias_rows(valid):
    row = lax.broadcasted_iota(jnp.int32, (16, SEG), 0)
    return jnp.where(row == 0, (1.0 - valid) * MASKED, 0.0).astype(BF16)


def dilated_body(
    proj_ref, tok_hbm, w_qkv_hbm, cot_ref, w_ref, valid_ref, back_out, key_out, query_ref, grad_ref,
    tok, weight_q, cot, weight_out, load_sem, msg, inbox, forwarded, acc, partial, back, key_half,
    send0, recv0, send1, recv1, send2, recv2, send3, recv3, pair_send, pair_recv,
):
    me = lax.axis_index("seq")
    dp = lax.axis_index("dp")
    chips = HEADS
    chip = me // 2
    core = me % 2
    partner = (dp, me + 1 - 2 * core)
    barrier = pltpu.get_barrier_semaphore()
    pl.semaphore_signal(barrier, inc=1, device_id=partner, device_id_type=MESH_ID)

    def greet(step, carry):
        target = (chip + step) % chips
        pl.semaphore_signal(
            barrier, inc=1, device_id=(dp, target * 2 + core), device_id_type=MESH_ID
        )
        return carry

    lax.fori_loop(1, chips, greet, 0)
    loads = [
        pltpu.make_async_copy(tok_hbm, tok, load_sem.at[0]),
        pltpu.make_async_copy(w_qkv_hbm.at[:, pl.ds(0, D)], weight_q, load_sem.at[1]),
        pltpu.make_async_copy(cot_ref, cot, load_sem.at[2]),
        pltpu.make_async_copy(w_ref, weight_out, load_sem.at[3]),
    ]
    for load in loads:
        load.start()

    def chip_copy(step, src, dst, send, recv):
        target = (chip + step) % chips
        return pltpu.make_async_remote_copy(
            src_ref=src(target), dst_ref=dst,
            send_sem=send.at[step], recv_sem=recv.at[step],
            device_id=(dp, target * 2 + core), device_id_type=MESH_ID,
        )

    def send_pairs(step):
        return chip_copy(step, lambda t: msg.at[0, t], inbox.at[0, chip], send0, recv0)

    def send_rows(step):
        return chip_copy(step, lambda t: msg.at[1, t], inbox.at[1, chip], send1, recv1)

    def send_back(step):
        return chip_copy(step, lambda t: back.at[t], back_out.at[chip], send2, recv2)

    def send_keys(step):
        return chip_copy(step, lambda t: key_half.at[t], key_out.at[chip], send3, recv3)

    lane = lax.broadcasted_iota(jnp.int32, (ROWS, 128), 1)
    blank = jnp.zeros((16, SEG), BF16)
    ones = one_rows()
    bias = bias_rows(valid_ref[...])
    batch = 4

    def rows(ref, offset, head):
        return ref[pl.ds(pl.multiple_of((offset + head) * HEAD_DIM, 16), HEAD_DIM)]

    def key_side(head):
        return jnp.concatenate(
            [rows(proj_ref, 0, head), rows(proj_ref, HEADS, head), bias, blank], axis=0
        )

    def pair_batch(at, carry):
        heads = [(chip + at * batch + i) % chips for i in range(batch)]
        packed = [dot(row_select(h), key_side(h), 1, 1).astype(BF16) for h in heads]
        for h, p in zip(heads, packed):
            msg[0, h] = p
        return carry

    lax.fori_loop(0, chips // batch, pair_batch, 0)
    pl.semaphore_wait(barrier, chips)

    def start_pairs(step, carry):
        send_pairs(step).start()
        return carry

    lax.fori_loop(1, chips, start_pairs, 0)
    inbox[0, chip] = msg[0, chip]
    for load in loads:
        load.wait()
    for at in range(0, D, 256):
        query_ref[at:at + 256] = dot(weight_q[:, at:at + 256], tok[...], 0, 1).astype(BF16)
        grad_ref[at:at + 256] = (
            dot(weight_out[at:at + 256], cot[...], 1, 1) * valid_ref[...]
        ).astype(BF16)

    def end_pairs(step, carry):
        send_pairs(step).wait()
        return carry

    lax.fori_loop(1, chips, end_pairs, 0)

    def pair_copy(at, src, dst):
        return pltpu.make_async_remote_copy(
            src_ref=src, dst_ref=dst, send_sem=pair_send.at[at], recv_sem=pair_recv.at[at],
            device_id=partner, device_id_type=MESH_ID,
        )

    forward = pair_copy(0, inbox.at[0], forwarded)
    forward.start()

    def select_batch(at, carry):
        steps = [at * batch + i for i in range(batch)]
        heads = [(chip + step) % chips for step in steps]
        key_sides = [key_side(h) for h in heads]
        queries = [
            dot(
                row_select(h),
                jnp.concatenate([rows(query_ref, 0, h), rows(grad_ref, 0, h), ones, blank], axis=0),
                1, 1,
            )
            for h in heads
        ]
        both = [
            jnp.concatenate(
                [
                    jnp.where((lane < 48) | (lane == 96), q, 0.0).astype(BF16),
                    jnp.where((lane >= 48) & (lane < 96), q, 0.0).astype(BF16),
                ],
                axis=0,
            )
            for q in queries
        ]
        scored = [dot(b, side, 1, 0) for b, side in zip(both, key_sides)]
        tops = [jnp.max(r[:ROWS], axis=1, keepdims=True) for r in scored]
        weights = [jnp.exp2(r[:ROWS] * SCALE2 - top * SCALE2) for r, top in zip(scored, tops)]
        totals = [jnp.sum(w, axis=1, keepdims=True) for w in weights]
        deltas = [jnp.sum(w * r[ROWS:], axis=1, keepdims=True) for w, r in zip(weights, scored)]
        for h, q, top, total, delta in zip(heads, queries, tops, totals, deltas):
            place = 97
            for value in (top * SCALE, total, delta):
                for part in three_parts(value):
                    q = jnp.where(lane == place, part, q)
                    place += 1
            msg[1, h] = q.astype(BF16)
        for step in steps:

            @pl.when(step > 0)
            def _(step=step):
                send_rows(step).start()

        return carry

    lax.fori_loop(0, chips // batch, select_batch, 0)
    inbox[1, chip] = msg[1, chip]

    def end_rows(step, carry):
        send_rows(step).wait()
        return carry

    lax.fori_loop(1, chips, end_rows, 0)
    half_keys = chips * ROWS
    queries_in = inbox[1].reshape(half_keys, 128)
    kv_own = inbox[0].reshape(half_keys, 128)
    forward.wait()
    kv = jnp.concatenate([kv_own, forwarded[...].reshape(half_keys, 128)], axis=0)
    chunk = 512
    q_lane = lax.broadcasted_iota(jnp.int32, (chunk, 128), 1)
    row = lax.broadcasted_iota(jnp.int32, (128, chunk), 0)
    key_lane = lax.broadcasted_iota(jnp.int32, (half_keys, 128), 1)

    def front(at):
        qg = queries_in[at:at + chunk]
        zero = jnp.zeros_like(qg)
        query = jnp.where((q_lane < 48) | (q_lane == 96), qg, zero)
        grad = jnp.where((q_lane >= 48) & (q_lane < 96), qg, zero)
        scores = dot(kv, query, 1, 1)
        raw_max = jnp.max(scores, axis=0, keepdims=True)
        weight = jnp.exp2(scores * SCALE2 - raw_max * SCALE2)
        return raw_max, weight, jnp.sum(weight, axis=0, keepdims=True), dot(kv, grad, 1, 1)

    def share(piece):
        span = pl.ds(piece * (half_keys // 4), half_keys // 4)
        return pair_copy(1 + piece, acc.at[1, span], partial.at[span])

    def start_range(copy, base, size):
        def start_one(i, carry):
            step = (base + (i + chip) % size - chip + chips) % chips

            @pl.when(step > 0)
            def _():
                copy(step).start()

            return carry

        lax.fori_loop(0, size, start_one, 0)

    cuts = list(range(0, half_keys, chunk))
    ready = front(cuts[0])
    for n, at in enumerate(cuts):
        raw_max, weight, glob_sum, dprob = ready
        if n + 1 < len(cuts):
            ready = front(cuts[n + 1])
        qg = queries_in[at:at + chunk]
        flipped = qg.astype(F32).T
        loc_max = flipped[97:98] + flipped[98:99] + flipped[99:100]
        loc_sum = flipped[100:101] + flipped[101:102] + flipped[102:103]
        loc_delta = flipped[103:104] + flipped[104:105] + flipped[105:106]
        glob_max = raw_max * SCALE
        top = jnp.maximum(glob_max, loc_max)
        log_total = top + jnp.log(
            loc_sum * jnp.exp(loc_max - top) + glob_sum * jnp.exp(glob_max - top)
        )
        probs = weight * jnp.exp(glob_max - log_total)
        half = probs.astype(BF16)
        out = dot(kv, half, 0, 0)
        delta = jnp.sum(out[48:96] * flipped[48:96], axis=0, keepdims=True)
        delta = delta + loc_delta * jnp.exp(loc_max - log_total)
        dscore = (probs * (dprob - delta)).astype(BF16)
        grad_q = dot(kv, dscore, 0, 0)
        hi, mid, low = three_parts(log_total)
        answer = jnp.where(row < 48, grad_q, jnp.where(row < 96, out, 0.0))
        answer = jnp.where(
            row == 96, hi, jnp.where(row == 97, mid, jnp.where(row == 98, low, answer))
        )
        back[at // ROWS:(at + chunk) // ROWS] = (
            answer.T.astype(BF16).reshape(chunk // ROWS, ROWS, 128)
        )
        start_range(send_back, at // ROWS, chunk // ROWS)
        for slot in (1, 0):
            span = slice(slot * half_keys, (slot + 1) * half_keys)
            term = jnp.where(
                key_lane < 48, dot(dscore[span], qg, 1, 0),
                jnp.where(key_lane < 96, dot(half[span], qg, 1, 0), 0.0),
            )
            if n == 0:
                acc[slot] = term
            else:
                acc[slot] += term
            if slot == 1 and n + 1 == len(cuts):
                for piece in range(4):
                    share(piece).start()

    back_out[chip] = back[chip]
    for piece in range(4):
        share(piece).wait()
        span = slice(piece * (half_keys // 4), (piece + 1) * (half_keys // 4))
        key_half[piece * 4:piece * 4 + 4] = (
            (acc[0, span] + partial[span]).astype(BF16).reshape(4, ROWS, 128)
        )
        start_range(send_keys, piece * 4, 4)
    key_out[chip] = key_half[chip]

    def end_back(step, carry):
        send_back(step).wait()
        send_keys(step).wait()
        return carry

    lax.fori_loop(1, chips, end_back, 0)


def dilated_level(projected, token_rows, w_qkv, cot_rows, w_out, valid):
    packed = jax.ShapeDtypeStruct((HEADS, ROWS, 128), BF16)
    half_keys = HEADS * ROWS
    semaphores = pltpu.SemaphoreType.DMA((HEADS,))
    return pl.pallas_call(
        dilated_body,
        out_shape=(packed, packed) + (jax.ShapeDtypeStruct((D, SEG), BF16),) * 2,
        in_specs=[
            pl.BlockSpec(memory_space=m) for m in (pltpu.VMEM,) + (pl.ANY,) * 4 + (pltpu.VMEM,)
        ],
        out_specs=[pl.BlockSpec(memory_space=pltpu.VMEM)] * 4,
        scratch_shapes=[
            pltpu.VMEM((SEG, D), BF16),
            pltpu.VMEM((D, D), BF16),
            pltpu.VMEM((SEG, D), BF16),
            pltpu.VMEM((D, D), BF16),
            pltpu.SemaphoreType.DMA((4,)),
            pltpu.VMEM((2, HEADS, ROWS, 128), BF16),
            pltpu.VMEM((2, HEADS, ROWS, 128), BF16),
            pltpu.VMEM((HEADS, ROWS, 128), BF16),
            pltpu.VMEM((2, half_keys, 128), F32),
            pltpu.VMEM((half_keys, 128), F32),
            pltpu.VMEM((HEADS, ROWS, 128), BF16),
            pltpu.VMEM((HEADS, ROWS, 128), BF16),
        ] + [semaphores] * 8 + [pltpu.SemaphoreType.DMA((5,))] * 2,
        compiler_params=pltpu.CompilerParams(
            collective_id=0, has_side_effects=True, vmem_limit_bytes=VMEM_LIMIT
        ),
    )(projected, token_rows, w_qkv, cot_rows, w_out, valid)


def finish_body(total_ref, last_ref, qkv_ref, out_ref):
    qkv_ref[...] = total_ref[:, 0].reshape(D, D).astype(F32).T

    @pl.when(pl.program_id(0) == 0)
    def _():
        out_ref[...] = last_ref[:, 0].reshape(D, D).astype(F32)


def finish(total):
    return pl.pallas_call(
        finish_body,
        grid=(3,),
        in_specs=[
            pl.BlockSpec((GROUPS, 1, GROUP_ROWS, D), lambda i: (0, i, 0, 0)),
            pl.BlockSpec((GROUPS, 1, GROUP_ROWS, D), lambda i: (0, 3, 0, 0)),
        ],
        out_specs=[pl.BlockSpec((D, D), lambda i: (0, i)), pl.BlockSpec((D, D), lambda i: (0, 0))],
        out_shape=[jax.ShapeDtypeStruct((D, 3 * D), F32), jax.ShapeDtypeStruct((D, D), F32)],
        compiler_params=pltpu.CompilerParams(vmem_limit_bytes=VMEM_LIMIT),
    )(total, total)


GROUPS = 4
GROUP_HEADS = HEADS // GROUPS
GROUP_ROWS = GROUP_HEADS * HEAD_DIM
PART = GROUP_ROWS // 3
LOCAL_CHUNK = 1024


def local_head(head, q_ref, k_ref, v_ref, g_ref, valid_ref, back_ref, key_ref):
    queries, keys, values, grads = q_ref[...], k_ref[...], v_ref[...], g_ref[...]
    keys_more = jnp.concatenate([keys, bias_rows(valid_ref[...])], axis=0)
    queries_more = jnp.concatenate([queries, one_rows()], axis=0)
    select = row_select(head)
    placed = dot(back_ref[0], select, 0, 0)
    key_placed = dot(key_ref[0], select, 0, 0)
    known = placed[96:97] + placed[97:98] + placed[98:99]
    sparse = lax.broadcasted_iota(jnp.int32, (1, LOCAL_CHUNK), 1) % RATE == head

    def front(at):
        cut = slice(at, at + LOCAL_CHUNK)
        scores = dot(keys_more, queries_more[:, cut], 0, 0)
        top = jnp.max(scores, axis=0, keepdims=True)
        weight = jnp.exp2(scores * SCALE2 - top * SCALE2)
        total = jnp.sum(weight, axis=0, keepdims=True)
        return top, weight, total, dot(values, grads[:, cut], 0, 0)

    cuts = list(range(0, SEG, LOCAL_CHUNK))
    context, grad_q = [], []
    grad_k = grad_v = 0.0
    ready = front(cuts[0])
    for n, at in enumerate(cuts):
        top, weight, total, dprob = ready
        if n + 1 < len(cuts):
            ready = front(cuts[n + 1])
        cut = slice(at, at + LOCAL_CHUNK)
        factor = jnp.where(sparse, jnp.exp(top * SCALE - known[:, cut]), 1.0 / total)
        probs = weight * factor
        half = probs.astype(BF16)
        out = dot(values, half, 1, 0) + placed[48:96, cut]
        grad = grads[:, cut]
        delta = jnp.sum(grad.astype(F32) * out, axis=0, keepdims=True)
        context.append((out * valid_ref[:, cut]).astype(BF16))
        dscore = (probs * (dprob - delta)).astype(BF16)
        grad_q.append(((dot(keys, dscore, 1, 0) + placed[0:48, cut]) * SCALE).astype(BF16))
        grad_k = grad_k + dot(dscore, queries[:, cut], 1, 1)
        grad_v = grad_v + dot(half, grad, 1, 1)
    grad_k = ((grad_k.T + key_placed[0:48]) * SCALE).astype(BF16)
    grad_v = (grad_v.T + key_placed[48:96]).astype(BF16)
    return (
        jnp.concatenate(context, axis=1), jnp.concatenate(grad_q, axis=1), grad_k, grad_v
    )


def local_body(
    q_ref, k_ref, v_ref, g_ref, valid_ref, back_ref, key_ref, tok_hbm, cot_hbm, w_hbm,
    att_ref, total_ref,
    tok_ref, cot_ref, w_ref, load_sem, rows_in, ctx, x, pair, got1, sum1, got2, got3, total,
    out_sem, pair_send, pair_recv, send, recv,
):
    head = pl.program_id(0)
    me = lax.axis_index("seq")
    z = lax.axis_index("dp")
    core = me % 2
    where = (me // 8, (me // 2) % 4, z)
    partner = (z, me + 1 - 2 * core)
    axes = [(0, 1, 2), (1, 2, 0), (2, 0, 1)]
    first = [where[axes[p][0]] for p in range(3)]
    second = [where[axes[p][1]] for p in range(3)]
    third = [where[axes[p][2]] for p in range(3)]
    parts, steps = range(3), (2, 1, 3)

    def peer(axis, coordinate):
        px, py, pz = [coordinate if axis == i else where[i] for i in range(3)]
        return (pz, (px * 4 + py) * 2 + core)

    def span(start, size, unit):
        return pl.ds(pl.multiple_of(start, unit), size)

    barrier = pltpu.get_barrier_semaphore()
    loads = [
        pltpu.make_async_copy(src, dst, load_sem.at[i])
        for i, (src, dst) in enumerate(((tok_hbm, tok_ref), (cot_hbm, cot_ref), (w_hbm, w_ref)))
    ]

    @pl.when(head == 0)
    def _():
        for load in loads:
            load.start()
        pl.semaphore_signal(barrier, inc=1, device_id=partner, device_id_type=MESH_ID)
        for axis in range(3):
            for step in range(1, 4):
                pl.semaphore_signal(
                    barrier, inc=1, device_id=peer(axis, (where[axis] + step) % 4), device_id_type=MESH_ID
                )

    @pl.when(head == GROUP_HEADS - 1)
    def _():
        for load in loads:
            load.wait()
        pl.semaphore_wait(barrier, 10)

    def remote(g, part, phase, step, src, dst):
        axis = axes[part][(0, 1, 2, 1, 0)[phase]]
        return pltpu.make_async_remote_copy(
            src_ref=src, dst_ref=dst,
            send_sem=send.at[g, part, phase, step - 1], recv_sem=recv.at[g, part, phase, step - 1],
            device_id=peer(axis, (where[axis] + step) % 4), device_id_type=MESH_ID,
        )

    def pair_out(g, part):
        rows = pl.ds(part * PART, PART)
        return pltpu.make_async_remote_copy(
            src_ref=x.at[g, pl.ds(2 * (1 - core), 2), rows], dst_ref=pair.at[g, :, rows],
            send_sem=pair_send.at[g, part], recv_sem=pair_recv.at[g, part],
            device_id=partner, device_id_type=MESH_ID,
        )

    def pair_back(g, part, arriving):
        half = pl.ds(2 * ((1 - core) if arriving else core), 2)
        block = total.at[g, half, pl.ds(part * PART, PART)]
        return pltpu.make_async_remote_copy(
            src_ref=block, dst_ref=block,
            send_sem=pair_send.at[g, 3 + part], recv_sem=pair_recv.at[g, 3 + part],
            device_id=partner, device_id_type=MESH_ID,
        )

    def quarter1(part, a):
        return 2 * core + a // 2, span(part * PART + (a % 2) * 32, 32, 32)

    def quarter2(b):
        return span((b // 2) * 16, 16, 16), span((b % 2) * 384, 384, 128)

    def shard(part, b):
        array, _ = quarter1(part, first[part])
        return (
            array,
            span(part * PART + (first[part] % 2) * 32 + (b // 2) * 16, 16, 16),
            span((b % 2) * 384, 384, 128),
        )

    def phase1(g, part, step):
        array, rows = quarter1(part, (first[part] + step) % 4)
        return remote(g, part, 0, step, x.at[g, array, rows], got1.at[g, part, step - 1])

    def phase2(g, part, step):
        rows, cols = quarter2((second[part] + step) % 4)
        return remote(g, part, 1, step, sum1.at[g, part, rows, cols], got2.at[g, part, step - 1])

    def phase3(g, part, step, arriving=False):
        slot = got3.at[g, part, (third[part] + (4 - step if arriving else 0)) % 4]
        return remote(g, part, 2, step, slot, slot)

    def phase4(g, part, step, arriving=False):
        array, rows, cols = shard(part, (second[part] + (4 - step if arriving else 0)) % 4)
        block = total.at[g, array, rows, cols]
        return remote(g, part, 3, step, block, block)

    def phase5(g, part, step, arriving=False):
        array, rows = quarter1(part, (first[part] + (4 - step if arriving else 0)) % 4)
        block = total.at[g, array, rows]
        return remote(g, part, 4, step, block, block)

    def write_back(g):
        return pltpu.make_async_copy(total.at[g], total_ref.at[g], out_sem.at[g])

    def stage1(g):
        for part in parts:
            pair_out(g, part).wait_recv()
            rows = slice(part * PART, (part + 1) * PART)
            for i in range(2):
                x[g, 2 * core + i, rows] = x[g, 2 * core + i, rows] + pair[g, i, rows]
            for step in steps:
                phase1(g, part, step).start()
        for part in parts:
            pair_out(g, part).wait_send()

    def stage2(g):
        for part in parts:
            for step in steps:
                phase1(g, part, step).wait_recv()
            array, rows = quarter1(part, first[part])
            sum1[g, part] = x[g, array, rows] + got1[g, part, 0] + got1[g, part, 1] + got1[g, part, 2]
            for step in steps:
                phase2(g, part, step).start()
        for part in parts:
            for step in steps:
                phase1(g, part, step).wait_send()

    def stage3(g):
        for part in parts:
            for step in steps:
                phase2(g, part, step).wait_recv()
            rows, cols = quarter2(second[part])
            got3[g, part, third[part]] = (
                sum1[g, part, rows, cols] + got2[g, part, 0] + got2[g, part, 1] + got2[g, part, 2]
            )
            for step in steps:
                phase3(g, part, step).start()
        for part in parts:
            for step in steps:
                phase2(g, part, step).wait_send()

    def stage4(g):
        for part in parts:
            for step in steps:
                phase3(g, part, step, True).wait_recv()
            array, rows, cols = shard(part, second[part])
            total[g, array, rows, cols] = (
                got3[g, part, 0] + got3[g, part, 1] + got3[g, part, 2] + got3[g, part, 3]
            ).astype(BF16)
            for step in steps:
                phase4(g, part, step).start()
        for part in parts:
            for step in steps:
                phase3(g, part, step).wait_send()

    def stage5(g):
        for part in parts:
            for step in steps:
                phase4(g, part, step, True).wait_recv()
            for step in steps:
                phase5(g, part, step).start()
        for part in parts:
            for step in steps:
                phase4(g, part, step).wait_send()

    def stage6(g):
        for part in parts:
            for step in steps:
                phase5(g, part, step, True).wait_recv()
            pair_back(g, part, False).start()
        for part in parts:
            for step in steps:
                phase5(g, part, step).wait_send()

    def stage7(g):
        for part in parts:
            pair_back(g, part, True).wait_recv()
        write_back(g).start()
        for part in parts:
            pair_back(g, part, False).wait_send()

    stages = (stage1, stage2, stage3, stage4, stage5, stage6, stage7)

    context, grad_q, grad_k, grad_v = local_head(
        head, q_ref, k_ref, v_ref, g_ref, valid_ref, back_ref, key_ref
    )
    here = span((head % GROUP_HEADS) * HEAD_DIM, HEAD_DIM, 16)
    rows_in[0, here] = grad_q
    rows_in[1, here] = grad_k
    rows_in[2, here] = grad_v
    rows_in[3, here] = context
    ctx[span(head * HEAD_DIM, HEAD_DIM, 16)] = context

    @pl.when(head % GROUP_HEADS == GROUP_HEADS - 1)
    def _():
        g = head // GROUP_HEADS

        def products(arrays):
            for i in arrays:
                x[g, i] = dot(rows_in[i], (cot_ref if i == 3 else tok_ref)[...], 1, 0)

        @pl.when(core == 0)
        def _():
            products((2, 3))

        @pl.when(core == 1)
        def _():
            products((0, 1))

        for part in parts:
            pair_out(g, part).start()

        @pl.when(core == 0)
        def _():
            products((0, 1))

        @pl.when(core == 1)
        def _():
            products((2, 3))

    for k, stage in enumerate(stages, 1):
        since = head - (GROUP_HEADS - 1) - k

        @pl.when((since >= 0) & (since % GROUP_HEADS == 0))
        def _(stage=stage, since=since):
            stage(since // GROUP_HEADS)

    @pl.when(head == HEADS - 1)
    def _():
        stage1(3)
        stage5(2)
        att_ref[...] = dot(ctx[...], w_ref[...], 0, 0).astype(BF16)
        stage2(3)
        stage6(2)
        stage3(3)
        stage7(2)
        stage4(3)
        stage5(3)
        stage6(3)
        stage7(3)
        for g in range(GROUPS):
            write_back(g).wait()


def shards(tokens, cotangent, lengths, w_qkv, w_out):
    token_rows = tokens[0]
    cot_rows = cotangent[0]
    first_pos = lax.axis_index("seq") * SEG
    row_valid = first_pos + jnp.arange(SEG, dtype=jnp.int32) < lengths[0]
    valid = row_valid.astype(F32)[None, :]
    projected = dot(w_qkv[:, D:], token_rows, 0, 1).astype(BF16)
    back_own, key_own, queries, grad_ctx = dilated_level(
        projected, token_rows, w_qkv, cot_rows, w_out, valid
    )

    def head_block(offset):
        return pl.BlockSpec((HEAD_DIM, SEG), lambda h: (h + offset, 0))

    head_specs = [head_block(0), head_block(0), head_block(HEADS), head_block(0)]
    heads = (queries, projected, projected, grad_ctx)
    packed = pl.BlockSpec((1, ROWS, 128), lambda h: (h, 0, 0))
    def whole(*shape):
        return pl.BlockSpec(shape, lambda h: (0,) * len(shape), pipeline_mode=pl.Buffered(1))

    attended, total = pl.pallas_call(
        local_body,
        grid=(HEADS,),
        in_specs=head_specs + [
            whole(1, SEG),
            packed,
            packed,
        ] + [pl.BlockSpec(memory_space=pl.ANY)] * 3,
        out_specs=[whole(SEG, D), pl.BlockSpec(memory_space=pl.ANY)],
        out_shape=[
            jax.ShapeDtypeStruct((SEG, D), BF16),
            jax.ShapeDtypeStruct((GROUPS, 4, GROUP_ROWS, D), BF16),
        ],
        scratch_shapes=[
            pltpu.VMEM((SEG, D), BF16),
            pltpu.VMEM((SEG, D), BF16),
            pltpu.VMEM((D, D), BF16),
            pltpu.SemaphoreType.DMA((3,)),
            pltpu.VMEM((4, GROUP_ROWS, SEG), BF16),
            pltpu.VMEM((D, SEG), BF16),
            pltpu.VMEM((GROUPS, 4, GROUP_ROWS, D), F32),
            pltpu.VMEM((GROUPS, 2, GROUP_ROWS, D), F32),
            pltpu.VMEM((GROUPS, 3, 3, 32, D), F32),
            pltpu.VMEM((GROUPS, 3, 32, D), F32),
            pltpu.VMEM((GROUPS, 3, 3, 16, 384), F32),
            pltpu.VMEM((GROUPS, 3, 4, 16, 384), F32),
            pltpu.VMEM((GROUPS, 4, GROUP_ROWS, D), BF16),
            pltpu.SemaphoreType.DMA((GROUPS,)),
            pltpu.SemaphoreType.DMA((GROUPS, 6)),
            pltpu.SemaphoreType.DMA((GROUPS, 6)),
            pltpu.SemaphoreType.DMA((GROUPS, 3, 5, 3)),
            pltpu.SemaphoreType.DMA((GROUPS, 3, 5, 3)),
        ],
        compiler_params=pltpu.CompilerParams(
            collective_id=2, has_side_effects=True, vmem_limit_bytes=60 * 2**20
        ),
    )(*heads, valid, back_own, key_own, token_rows, cot_rows, w_out)

    grad_qkv, grad_out = finish(total)
    return attended[None], grad_qkv, grad_out


def solution(mesh):
    return jax.shard_map(
        shards,
        mesh=mesh,
        in_specs=(P("dp", "seq", None), P("dp", "seq", None), P("dp"), P(), P()),
        out_specs=(P("dp", "seq", None), P(), P()),
        check_vma=False,
    )
```
